256 devices in a mesh: seq: 64 (over x, z, core), head: 4 (over y).
Axes of the slice: x: 4, y: 4, z: 8, core: 2. Of those that a mesh axis runs over, the one named last changes fastest.
Arguments:
- mention_queries: bfloat16 [2048, 4096], P(('seq', 'head')), may hold values from -6 to 6
- pack_keys: bfloat16 [65536, 1024], P(('seq', 'head')), may hold values from -6 to 6
- pack_values: bfloat16 [65536, 1024], P(('seq', 'head')), may hold values from -6 to 6
- desc_keys: bfloat16 [512, 32, 1024], P('seq', None, 'head'), may hold values from -6 to 6
- desc_values: bfloat16 [512, 32, 1024], P('seq', None, 'head'), may hold values from -6 to 6
- desc_lengths: int32 [512], replicated, may hold values from 1 to 32
- block_lists: int32 [128, 32], P('seq'), may hold values from 0 to 511, as said below
- block_home: int32 [512], replicated, may hold values from 0 to 511, as said below
- mention_positions: int32 [2048], P('seq'), may hold values from 0 to 511, as said below
- entity_table: bfloat16 [1024, 4096], P(None, 'head'), may hold values from -6 to 6
- teacher_ids: int32 [2048, 16], P('seq'), may hold values from 0 to 1023, all different within a row
- teacher_logits: float32 [2048, 16], P('seq'), may hold values from -260 to 260
Outputs:
- grad_queries: bfloat16 [2048, 4096], P('seq', 'head')
- grad_pack_keys: bfloat16 [65536, 1024], P('seq', 'head')
- grad_pack_values: bfloat16 [65536, 1024], P('seq', 'head')
- grad_desc_keys: float32 [512, 32, 1024], P('seq', None, 'head')
- grad_desc_values: float32 [512, 32, 1024], P('seq', None, 'head')
- divergence: float32 [2048], P('seq')
The draws below stay inside these ranges and needn't reach their ends.
Inputs may be any that keep to these rules, and one draw needn't show every extreme that they name: A permutation: block b lies in row block_home[b] of desc_keys. `block_lists`: one stretch lists distinct blocks; over the stretches of one index of seq the ids are distinct; at most 2 of them lie (by block_home) in the rows of any one index of seq, and for some index of seq exactly 2 do. `mention_positions`: the mentions of one stretch are at distinct positions.
All inputs are finite; a program needn't handle non-finite values.
Results may differ from the reference program's by a relative error of at most 0.029.
Values may be sent and summed in bfloat16 or wider, within the bound.
No kernel may reach another device: no remote copies, remote signals or barrier semaphores. Data moves between devices by JAX's collectives and lax.ppermute only.
A program may use at most 128 MiB of HBM per device.

```python
import jax
import jax.numpy as jnp
from jax import lax

HEADS = 32
KV_HEADS = 8
HEAD_DIM = 128
STRETCH = 512
DBLK = 32
CAP = 2
TOPK = 16
STRETCH_SEQ = 2
MEN_CH = 16
BLK_DEV = 8
ENT = 1024
LIST = 32
STRETCHES = 128
TOKENS = 65536
MENTIONS = 2048
NBLK = 512
N_SEQ = 64


def request_plan(key):
    hot_owner = jax.random.randint(jax.random.fold_in(key, 101), (), 0, N_SEQ)
    home = jax.random.permutation(jax.random.fold_in(key, 102), NBLK).astype(jnp.int32)
    block_at = jnp.argsort(home, stable=True).astype(jnp.int32)
    slots = N_SEQ * CAP
    wanted = STRETCH_SEQ * LIST

    def one_index(seq_index):
        inner = jax.random.fold_in(jax.random.fold_in(key, 103), seq_index)
        codes = jnp.arange(slots, dtype=jnp.int32)
        owner_code = codes // CAP
        slot_code = codes % CAP
        noise = jax.random.permutation(jax.random.fold_in(inner, 1), slots).astype(jnp.int32)
        score = jnp.where(owner_code == hot_owner, -1 - slot_code, noise)
        order = jnp.argsort(score, stable=True)[:wanted]
        owners = owner_code[order]
        slot_ids = slot_code[order]
        bases = jax.random.randint(jax.random.fold_in(inner, 2), (N_SEQ,), 0, BLK_DEV)
        local = (bases[owners] + slot_ids) % BLK_DEV
        stored = owners * BLK_DEV + local
        shuffle = jax.random.permutation(jax.random.fold_in(inner, 3), wanted)
        return block_at[stored[shuffle]]
    lists = jax.vmap(one_index)(jnp.arange(N_SEQ, dtype=jnp.int32))
    return (home, lists.reshape(STRETCH_SEQ * N_SEQ, LIST).astype(jnp.int32))


def draw_block_home(key, part):
    home, lists = request_plan(key)
    return home


def draw_block_lists(key, part):
    home, lists = request_plan(key)
    return lists


def draw_desc_lengths(key, part):
    key = jax.random.fold_in(key, 21)
    lengths = jax.random.randint(key, (NBLK,), 1, DBLK + 1)
    return lengths.at[0].set(DBLK).at[1].set(1).astype(jnp.int32)


def draw_mention_positions(key, part):
    key = jax.random.fold_in(key, 41)

    def one_stretch(index):
        inner = jax.random.fold_in(key, index)
        middle = jax.random.permutation(jax.random.fold_in(inner, 1), STRETCH - 2)[:MEN_CH - 2] + 1
        joined = jnp.concatenate([jnp.array([0, STRETCH - 1], jnp.int32), middle.astype(jnp.int32)])
        return joined[jax.random.permutation(jax.random.fold_in(inner, 2), MEN_CH)]
    return jax.vmap(one_stretch)(jnp.arange(STRETCHES, dtype=jnp.int32)).reshape(MENTIONS).astype(jnp.int32)


def draw_mention_queries(key, part):
    key = jax.random.fold_in(key, 51)
    shape = (MENTIONS, HEADS * HEAD_DIM)
    base = jax.random.normal(jax.random.fold_in(key, 1), shape, jnp.float32)
    return jnp.clip(base, -6.0, 6.0).astype(jnp.bfloat16)


def draw_desc_keys(key, part):
    key = jax.random.fold_in(key, 61)
    shape = (NBLK, DBLK, KV_HEADS * HEAD_DIM)
    base = jax.random.normal(jax.random.fold_in(key, 1), shape, jnp.float32)
    return jnp.clip(base, -6.0, 6.0).astype(jnp.bfloat16)


def draw_teacher_logits(key, part):
    key = jax.random.fold_in(key, 71)
    shape = (MENTIONS, TOPK)
    base = jnp.clip(3.0 * jax.random.normal(jax.random.fold_in(key, 1), shape, jnp.float32), -12.0, 12.0)
    return base.astype(jnp.float32)


def block_levels(own_key, dims, pieces, low, largest):
    level, own = 1.0, jax.random.fold_in(own_key, 6)
    for position, shards_of in pieces:
        draws = jnp.exp(jax.random.uniform(jax.random.fold_in(own, position), (shards_of,), jnp.float32, low / len(pieces), largest / len(pieces)))
        level = level * jnp.repeat(draws, dims[position] // shards_of).reshape([-1 if axis == position else 1 for axis in range(len(dims))])
    return level


def different_ones(stream_key, rows, count, top, lift):
    order = jax.random.permutation(jax.random.fold_in(stream_key, 1), count)
    pull = order
    for power in range(3):
        pull = pull * pull // count
    pull = pull * lift // count
    lots = jax.random.randint(jax.random.fold_in(stream_key, 2), (rows, count), 0, 4096) + pull
    fixed_rows = jax.random.permutation(jax.random.fold_in(stream_key, 3), rows)[jnp.arange(count) % rows]
    lots = jnp.where(jnp.arange(rows)[:, None] == fixed_rows[None, :], 1 << 14, lots)
    merit = lots * count + jnp.arange(count)
    return lax.top_k(merit.astype(jnp.int32), top)[1].astype(jnp.int32)


def gaussian(key, dims, spread, reach, shards=(), kind=jnp.bfloat16):
    drawn = spread * jax.random.normal(key, dims, jnp.float32)
    if shards:
        drawn = drawn * block_levels(key, dims, shards, -0.22, 0.18)
    return jnp.clip(drawn, -reach, reach).astype(kind)


def setup_inputs(seed: int = 0) -> dict:
    arg_keys = jax.random.split(jax.random.key(seed), 13)
    return {
        "mention_queries": draw_mention_queries(jax.random.fold_in(arg_keys[12], 71), 0),
        "pack_keys": gaussian(arg_keys[1], (TOKENS, KV_HEADS * HEAD_DIM), 1.0, 6.0, ((0, 256),)),
        "pack_values": gaussian(arg_keys[2], (TOKENS, KV_HEADS * HEAD_DIM), 1.0, 6.0, ((0, 256),)),
        "desc_keys": draw_desc_keys(jax.random.fold_in(arg_keys[12], 71), 0),
        "desc_values": gaussian(arg_keys[4], (NBLK, DBLK, KV_HEADS * HEAD_DIM), 1.0, 6.0, ((0, 64), (2, 4))),
        "desc_lengths": draw_desc_lengths(jax.random.fold_in(arg_keys[12], 71), 0),
        "block_lists": draw_block_lists(jax.random.fold_in(arg_keys[12], 71), 0),
        "block_home": draw_block_home(jax.random.fold_in(arg_keys[12], 71), 0),
        "mention_positions": draw_mention_positions(jax.random.fold_in(arg_keys[12], 71), 0),
        "entity_table": gaussian(arg_keys[9], (ENT, HEADS * HEAD_DIM), 1.0, 6.0, ((1, 4),)),
        "teacher_ids": different_ones(arg_keys[10], MENTIONS, ENT, TOPK, 256),
        "teacher_logits": draw_teacher_logits(jax.random.fold_in(arg_keys[12], 71), 0),
    }


def lowered(values):
    return lax.optimization_barrier(values.astype(jnp.bfloat16)).astype(jnp.float32)


def reference(mention_queries, pack_keys, pack_values, desc_keys, desc_values, desc_lengths, block_lists, block_home, mention_positions, entity_table, teacher_ids, teacher_logits):
    scale = HEAD_DIM ** -0.5
    group = HEADS // KV_HEADS
    kv_cols = KV_HEADS * HEAD_DIM
    span = LIST * DBLK

    def step(carry, index):
        grad_dk, grad_dv = carry
        queries = lax.dynamic_slice_in_dim(mention_queries, index * MEN_CH, MEN_CH, 0)
        positions = lax.dynamic_slice_in_dim(mention_positions, index * MEN_CH, MEN_CH, 0)
        entity_ids = lax.dynamic_slice_in_dim(teacher_ids, index * MEN_CH, MEN_CH, 0)
        teacher = lax.dynamic_slice_in_dim(teacher_logits, index * MEN_CH, MEN_CH, 0)
        listed = lax.dynamic_slice_in_dim(block_lists, index, 1, 0)[0]
        stored = jnp.take(block_home, listed).astype(jnp.int32)
        lengths = jnp.take(desc_lengths, stored)
        desc_k = jnp.take(desc_keys, stored, axis=0).reshape(span, kv_cols)
        desc_v = jnp.take(desc_values, stored, axis=0).reshape(span, kv_cols)
        self_k = lax.dynamic_slice_in_dim(pack_keys, index * STRETCH, STRETCH, 0)
        self_v = lax.dynamic_slice_in_dim(pack_values, index * STRETCH, STRETCH, 0)
        keys = jnp.concatenate([desc_k, self_k], 0).astype(jnp.float32).reshape(-1, KV_HEADS, HEAD_DIM)
        values = jnp.concatenate([desc_v, self_v], 0).astype(jnp.float32).reshape(-1, KV_HEADS, HEAD_DIM)
        desc_mask = (jnp.arange(DBLK)[None, :] < lengths[:, None]).reshape(span)
        self_mask = jnp.arange(STRETCH)[None, :] <= positions[:, None]
        mask = jnp.concatenate([jnp.broadcast_to(desc_mask[None, :], (MEN_CH, span)), self_mask], 1)
        query_f = queries.astype(jnp.float32).reshape(MEN_CH, KV_HEADS, group, HEAD_DIM)
        scores = jnp.einsum('mkgd,lkd->mkgl', query_f, keys) * scale
        scores = jnp.where(mask[:, None, None, :], scores, -1e30)
        probs = jax.nn.softmax(scores, axis=-1)
        probs_low = lowered(probs)
        attended = lowered(jnp.einsum('mkgl,lkd->mkgd', probs_low, values).reshape(MEN_CH, -1))
        table = jnp.take(entity_table, entity_ids, axis=0).astype(jnp.float32)
        logits = jnp.einsum('mq,mtq->mt', attended, table)
        target = jax.nn.softmax(teacher, axis=-1)
        kl_terms = jnp.sum(target * (jax.nn.log_softmax(teacher, axis=-1) - jax.nn.log_softmax(logits, axis=-1)), axis=-1)
        grad_logits = jax.nn.softmax(logits, axis=-1) - target
        grad_att = lowered(jnp.einsum('mt,mtq->mq', grad_logits, table)).reshape(MEN_CH, KV_HEADS, group, HEAD_DIM)
        grad_probs = jnp.einsum('mkgd,lkd->mkgl', grad_att, values)
        center = jnp.sum(probs * grad_probs, axis=-1, keepdims=True)
        grad_scores = lowered(probs * (grad_probs - center))
        grad_q = (jnp.einsum('mkgl,lkd->mkgd', grad_scores, keys) * scale).reshape(MEN_CH, -1).astype(jnp.bfloat16)
        grad_keys = (jnp.einsum('mkgl,mkgd->lkd', grad_scores, query_f) * scale).reshape(-1, kv_cols)
        grad_values = jnp.einsum('mkgl,mkgd->lkd', probs_low, grad_att).reshape(-1, kv_cols)
        grad_dk = grad_dk.at[stored].add(grad_keys[:span].reshape(LIST, DBLK, kv_cols))
        grad_dv = grad_dv.at[stored].add(grad_values[:span].reshape(LIST, DBLK, kv_cols))
        outputs = (grad_q, grad_keys[span:].astype(jnp.bfloat16), grad_values[span:].astype(jnp.bfloat16), kl_terms)
        return (grad_dk, grad_dv), outputs

    empty = jnp.zeros((NBLK, DBLK, kv_cols), jnp.float32)
    (grad_dk, grad_dv), (grad_q, grad_pk, grad_pv, kl_all) = lax.scan(step, (empty, empty), jnp.arange(STRETCHES, dtype=jnp.int32))
    return (grad_q.reshape(MENTIONS, -1), grad_pk.reshape(TOKENS, -1), grad_pv.reshape(TOKENS, -1), grad_dk, grad_dv, kl_all.reshape(MENTIONS))
```

```python
import functools

import jax
import jax.numpy as jnp
from jax import lax
from jax.experimental import pallas as pl
from jax.experimental.pallas import tpu as pltpu
from jax.sharding import PartitionSpec as P

HEAD_DIM = 128
SCALE = HEAD_DIM ** (-0.5)
NX, NZ, NC, NH = 4, 8, 2, 4
GROUP = 4
KV = 2
HEADS = GROUP * KV
COLS = HEADS * HEAD_DIM
WIDE = COLS + 128
DBLK = 32
BLK = 8
OWN = BLK * DBLK
CHIP = NC * OWN
MEN = 32
MEN_CH = 16
STRETCH = 512
LISTED = 64
SLOTS = 2 * NZ * NC
SPAN = SLOTS * DBLK
LOW = -1e30
F32 = jnp.float32
BF16 = jnp.bfloat16
NT = (((1,), (1,)), ((), ()))
TN = (((0,), (0,)), ((), ()))
VMEM_BYTES = 40 * 1024 * 1024


def pairs(move):
    out = []
    for x in range(NX):
        for z in range(NZ):
            for c in range(NC):
                tx, tz, tc = move(x, z, c)
                out.append(((x * NZ + z) * NC + c, ((tx % NX) * NZ + tz % NZ) * NC + tc))
    return out


def shift_x(value, step):
    return lax.ppermute(value, "seq", pairs(lambda x, z, c: (x + step, z, c)))


def shift_z(value, step):
    return lax.ppermute(value, "seq", pairs(lambda x, z, c: (x, z + step, c)))


def shift_z_apart(value):
    return lax.ppermute(value, "seq", pairs(lambda x, z, c: (x, z + 1 - 2 * c, c)))


def swap(value):
    return lax.ppermute(value, "seq", pairs(lambda x, z, c: (x, z, 1 - c)))


def shift_head(value, step):
    return lax.ppermute(value, "head", [(i, (i + step) % NH) for i in range(NH)])


def dot(left, right, dims=(((1,), (0,)), ((), ()))):
    return lax.dot_general(left, right, dims, preferred_element_type=F32)


def head_cols(head):
    return slice(head * HEAD_DIM, (head + 1) * HEAD_DIM)


def call(kernel, out_shape, operands, smem=(), scratch=(), flops=0, moved=0):
    specs = [
        pl.BlockSpec(memory_space=pltpu.SMEM if i in smem else pltpu.VMEM)
        for i in range(len(operands))
    ]
    one = pl.BlockSpec(memory_space=pltpu.VMEM)
    return pl.pallas_call(
        kernel,
        out_shape=out_shape,
        in_specs=specs,
        out_specs=jax.tree.map(lambda _: one, out_shape),
        scratch_shapes=list(scratch),
        compiler_params=pltpu.CompilerParams(vmem_limit_bytes=VMEM_BYTES),
        cost_estimate=pl.CostEstimate(flops=flops, bytes_accessed=moved, transcendentals=0),
    )(*operands)


def stack_heads(ref, index, kv, rows):
    take = (lambda h: ref[rows, head_cols(h)]) if index is None else (lambda h: ref[index, rows, head_cols(h)])
    return jnp.concatenate([take(kv * GROUP + g) for g in range(GROUP)], 0)


def stack_numbers(tile, kv):
    return jnp.concatenate([tile[:, kv * GROUP + g : kv * GROUP + g + 1] for g in range(GROUP)], 0)


def unpack_numbers(tile):
    first = tile + pltpu.roll(tile, 120, 1) + pltpu.roll(tile, 112, 1)
    second = pltpu.roll(tile, 104, 1) + pltpu.roll(tile, 96, 1) + pltpu.roll(tile, 88, 1)
    return first, second


def three_parts(value):
    high = value.astype(BF16).astype(F32)
    rest = value - high
    middle = rest.astype(BF16).astype(F32)
    return high, middle, (rest - middle).astype(BF16).astype(F32)


def attend(scores, values):
    top = jnp.max(scores, axis=1, keepdims=True)
    weights = jnp.exp(scores - top)
    total = jnp.sum(weights, axis=1, keepdims=True)
    return dot(weights.astype(BF16), values) / total, top + jnp.log(total)


def self_forward(queries, keys, values, positions, out):
    lane = lax.broadcasted_iota(jnp.int32, (MEN_CH, 128), 1)
    token = lax.broadcasted_iota(jnp.int32, (GROUP * MEN_CH, STRETCH), 1)
    for t in range(2):
        rows = slice(t * MEN_CH, (t + 1) * MEN_CH)
        span = slice(t * STRETCH, (t + 1) * STRETCH)
        place = jnp.concatenate([positions[rows, :]] * GROUP, 0)
        tile = jnp.zeros((MEN_CH, 128), F32)
        for kv in range(KV):
            q = stack_heads(queries, None, kv, rows)
            scores = dot(q, keys[span, head_cols(kv)], NT) * SCALE
            scores = jnp.where(token <= place, scores, LOW)
            att, lse = attend(scores, values[span, head_cols(kv)])
            for g in range(GROUP):
                head = kv * GROUP + g
                part = slice(g * MEN_CH, (g + 1) * MEN_CH)
                out[rows, head_cols(head)] = att[part]
                tile = jnp.where(lane == head, lse[part], tile)
        out[rows, COLS:WIDE] = tile


def self_backward(queries, keys, values, positions, message, out_q, out_k, out_v):
    token = lax.broadcasted_iota(jnp.int32, (GROUP * MEN_CH, STRETCH), 1)
    for t in range(2):
        rows = slice(t * MEN_CH, (t + 1) * MEN_CH)
        span = slice(t * STRETCH, (t + 1) * STRETCH)
        place = jnp.concatenate([positions[rows, :]] * GROUP, 0)
        lse, center = unpack_numbers(message[rows, COLS:WIDE].astype(F32))
        for kv in range(KV):
            q = stack_heads(queries, None, kv, rows)
            grad = stack_heads(message, None, kv, rows)
            key = keys[span, head_cols(kv)]
            value = values[span, head_cols(kv)]
            scores = dot(q, key, NT) * SCALE
            scores = jnp.where(token <= place, scores, LOW)
            probs = jnp.exp(scores - stack_numbers(lse, kv))
            grad_scores = probs * (dot(grad, value, NT) - stack_numbers(center, kv))
            low = grad_scores.astype(BF16)
            grad_q = dot(low, key) * SCALE
            for g in range(GROUP):
                out_q[rows, head_cols(kv * GROUP + g)] = grad_q[g * MEN_CH : (g + 1) * MEN_CH]
            out_k[span, head_cols(kv)] = (dot(low, q, TN) * SCALE).astype(BF16)
            out_v[span, head_cols(kv)] = dot(probs.astype(BF16), grad, TN).astype(BF16)


def masked(scores, bias):
    four = scores.reshape(GROUP, 2, MEN_CH, SPAN) + bias[None, :, None, :]
    return four.reshape(GROUP * MEN, SPAN)


def node_forward(row_k, row_v, queries, bias, first, r1, r2, r3, s1, s2, s3, far, far_s, out, out_k, out_v, pool):
    half = NZ * CHIP
    for i, piece in enumerate((first, r1, r2, r3)):
        pool[i * CHIP : (i + 1) * CHIP, :] = piece[0]
        pool[half + i * CHIP : half + (i + 1) * CHIP, :] = piece[1]
    for i, piece in enumerate((s1, s2, s3)):
        pool[(4 + i) * CHIP : (5 + i) * CHIP, :] = piece[1]
        pool[half + (4 + i) * CHIP : half + (5 + i) * CHIP, :] = piece[0]
    pool[7 * CHIP : 8 * CHIP, :] = far[...]
    pool[half + 7 * CHIP : half + 8 * CHIP, :] = far_s[...]
    lane = lax.broadcasted_iota(jnp.int32, (MEN, 128), 1)
    for r in range(NX):
        for j in range(SLOTS):
            rows = slice(j * DBLK, (j + 1) * DBLK)
            out_k[r, rows, :] = pool[pl.ds(pl.multiple_of(row_k[r, j], DBLK), DBLK), :]
            out_v[r, rows, :] = pool[pl.ds(pl.multiple_of(row_v[r, j], DBLK), DBLK), :]
        tile = jnp.zeros((MEN, 128), F32)
        for kv in range(KV):
            q = stack_heads(queries, r, kv, slice(None))
            scores = masked(dot(q, out_k[r, :, head_cols(kv)], NT) * SCALE, bias[r])
            att, lse = attend(scores, out_v[r, :, head_cols(kv)])
            for g in range(GROUP):
                head = kv * GROUP + g
                part = slice(g * MEN, (g + 1) * MEN)
                out[r, :, head_cols(head)] = att[part]
                tile = jnp.where(lane == head, lse[part], tile)
        out[r, :, COLS:WIDE] = tile


def node_backward(queries, message, bias, keys, values, out):
    for r in range(NX):
        lse, center = unpack_numbers(message[r, :, COLS:WIDE].astype(F32))
        for kv in range(KV):
            q = stack_heads(queries, r, kv, slice(None))
            grad = stack_heads(message, r, kv, slice(None))
            key = keys[r, :, head_cols(kv)]
            scores = masked(dot(q, key, NT) * SCALE, bias[r])
            probs = jnp.exp(scores - stack_numbers(lse, kv))
            grad_probs = dot(grad, values[r, :, head_cols(kv)], NT)
            low = (probs * (grad_probs - stack_numbers(center, kv))).astype(BF16)
            grad_q = (dot(low, key) * SCALE).astype(BF16)
            for g in range(GROUP):
                out[r, :, head_cols(kv * GROUP + g)] = grad_q[g * MEN : (g + 1) * MEN]


def entity_forward(own, y1, y2, y3, local, table, ids, out_att, out_lse, out_logits):
    parts = (own, y1, y2, y3, local)
    lses = [part[:, COLS:WIDE] for part in parts]
    top = functools.reduce(jnp.maximum, lses)
    weights = [jnp.exp(lse - top) for lse in lses]
    total = functools.reduce(jnp.add, weights)
    out_lse[...] = top + jnp.log(total)
    weights = [weight / total for weight in weights]
    lows = []
    for head in range(HEADS):
        att = functools.reduce(
            jnp.add, [part[:, head_cols(head)] * w[:, head : head + 1] for part, w in zip(parts, weights)]
        )
        out_att[:, head_cols(head)] = att
        lows.append(att.astype(BF16))
    every = dot(jnp.concatenate(lows, 1), table[...], NT)
    entity = lax.broadcasted_iota(jnp.int32, every.shape, 1)
    lane = lax.broadcasted_iota(jnp.int32, (MEN, 128), 1)
    logits = jnp.zeros((MEN, 128), F32)
    for k in range(ids.shape[1]):
        picked = jnp.sum(jnp.where(entity == ids[:, k : k + 1], every, 0.0), axis=1, keepdims=True)
        logits = jnp.where(lane == k, picked, logits)
    out_logits[...] = logits


def log_softmax(values, live):
    values = jnp.where(live, values, LOW)
    values = values - jnp.max(values, axis=1, keepdims=True)
    return values - jnp.log(jnp.sum(jnp.exp(values), axis=1, keepdims=True))


def entity_backward(l0, l1, l2, l3, teacher, ids, table, att, lse, out, out_div):
    count = ids.shape[1]
    lane = lax.broadcasted_iota(jnp.int32, (MEN, 128), 1)
    live = lane < count
    log_model = log_softmax((l0[...] + l2[...]) + (l1[...] + l3[...]), live)
    log_target = log_softmax(teacher[...], live)
    target = jnp.where(live, jnp.exp(log_target), 0.0)
    terms = jnp.where(live, target * (log_target - log_model), 0.0)
    out_div[...] = jnp.broadcast_to(jnp.sum(terms, axis=1, keepdims=True), (MEN, 128))
    grad_logits = jnp.where(live, jnp.exp(log_model), 0.0) - target
    entity = lax.broadcasted_iota(jnp.int32, (MEN, table.shape[0]), 1)
    spread = jnp.zeros((MEN, table.shape[0]), F32)
    for k in range(count):
        spread = jnp.where(entity == ids[:, k : k + 1], grad_logits[:, k : k + 1], spread)
    high, middle, low = three_parts(spread)
    three = dot(jnp.concatenate([high, middle, low], 0).astype(BF16), table[...])
    grad = (three[:MEN] + three[MEN : 2 * MEN] + three[2 * MEN :]).astype(BF16)
    out[:, :COLS] = grad
    center = jnp.zeros((MEN, 128), F32)
    for head in range(HEADS):
        product = grad[:, head_cols(head)].astype(F32) * att[:, head_cols(head)]
        center = jnp.where(lane == head, jnp.sum(product, axis=1, keepdims=True), center)
    numbers = jnp.zeros((MEN, 128), F32)
    for i, part in enumerate(three_parts(jnp.where(lane < HEADS, lse[...], 0.0)) + three_parts(center)):
        numbers = numbers + (pltpu.roll(part, i * HEADS, 1) if i else part)
    out[:, COLS:WIDE] = numbers.astype(BF16)


def owner_kernel(count, has_start, chip, keys, values, *refs):
    refs = list(refs)
    start = (refs.pop(0), refs.pop(0)) if has_start else None
    qs = [refs.pop(0) for _ in range(count)]
    gs = [refs.pop(0) for _ in range(count)]
    out_k, out_v, q_all, g_all = refs
    at = 0
    for q, g in zip(qs, gs):
        q_all[at : at + q.shape[0], :] = q[...]
        g_all[at : at + q.shape[0], :] = g[...]
        at += q.shape[0]
    if start is None:
        out_k[...] = jnp.zeros_like(out_k)
        out_v[...] = jnp.zeros_like(out_v)
    else:
        out_k[...] = start[0][...]
        out_v[...] = start[1][...]
    blocks = CHIP // DBLK
    base = (chip[0] * blocks).astype(F32)
    block = lax.broadcasted_iota(jnp.int32, (blocks, 128), 0).astype(F32) + base
    same = (
        lax.broadcasted_iota(jnp.int32, (128, 128), 0) // MEN_CH
        == lax.broadcasted_iota(jnp.int32, (128, 128), 1) // MEN_CH
    )
    same = jnp.where(same, 1.0, 0.0).astype(BF16)

    def step(i, carry):
        rows = pl.ds(pl.multiple_of(i * 128, 128), 128)
        lists = jnp.transpose(q_all[rows, COLS:WIDE].astype(F32))
        hit = ((lists[0:1] * BLK + lists[2:3]) == block) | ((lists[1:2] * BLK + lists[3:4]) == block)
        listed = dot(jnp.where(hit, 1.0, 0.0).astype(BF16), same) > 0.5
        numbers = jnp.transpose(g_all[rows, COLS:WIDE].astype(F32))
        lse = numbers[0:8] + numbers[8:16] + numbers[16:24]
        center = numbers[24:32] + numbers[32:40] + numbers[40:48]
        for kv in range(KV):
            heads = range(kv * GROUP, (kv + 1) * GROUP)
            q = jnp.concatenate([q_all[rows, head_cols(h)] for h in heads], 0)
            g = jnp.concatenate([g_all[rows, head_cols(h)] for h in heads], 0)
            offset = jnp.concatenate([jnp.where(listed, -lse[h : h + 1], LOW) for h in heads], 1)
            middle = jnp.concatenate([center[h : h + 1] for h in heads], 1)
            scores = dot(keys[:, head_cols(kv)], q, NT) * SCALE
            scores = scores.reshape(blocks, DBLK, scores.shape[1]) + offset[:, None, :]
            probs = jnp.exp(scores.reshape(CHIP, scores.shape[2]))
            grad_probs = dot(values[:, head_cols(kv)], g, NT)
            low = (probs * (grad_probs - middle)).astype(BF16)
            out_v[:, head_cols(kv)] += dot(probs.astype(BF16), g)
            out_k[:, head_cols(kv)] += dot(low, q)
        return carry

    lax.fori_loop(0, at // 128, step, 0)


def owner_part(chip, keys, values, start, qs, gs):
    shape = jax.ShapeDtypeStruct((CHIP, KV * HEAD_DIM), F32)
    rows = sum(q.shape[0] for q in qs)
    operands = [chip, keys, values] + list(start or ()) + list(qs) + list(gs)
    return call(
        functools.partial(owner_kernel, len(qs), start is not None),
        (shape, shape),
        operands,
        smem=(0,),
        scratch=[pltpu.VMEM((rows, WIDE), BF16), pltpu.VMEM((rows, WIDE), BF16)],
        flops=8 * rows * HEADS * CHIP * HEAD_DIM,
        moved=4 * rows * WIDE + 12 * CHIP * KV * HEAD_DIM,
    )


def around_z(value):
    up, down = [value], [value]
    for _ in range(3):
        up.append(shift_z(up[-1], 1))
        down.append(shift_z(down[-1], -1))
    half = value.shape[0] // 2
    far = (shift_z(up[-1][:half], 1), shift_z(down[-1][half:], -1))
    return up[1:], down[1:], far


def per_device(
    mention_queries,
    pack_keys,
    pack_values,
    desc_keys,
    desc_values,
    desc_lengths,
    block_lists,
    block_home,
    mention_positions,
    entity_table,
    teacher_ids,
    teacher_logits,
):
    me = lax.axis_index("seq")
    my_x, my_z, my_c = me // (NZ * NC), (me // NC) % NZ, me % NC
    core0 = my_c == 0

    listed = block_lists.reshape(MEN, 2)
    home = jnp.take(block_home, listed)
    lengths = jnp.take(desc_lengths, home)
    extra = jnp.concatenate([home // BLK, home % BLK, lengths], 1).astype(BF16)
    extra = jnp.pad(extra, ((0, 0), (0, 128 - extra.shape[1])))
    queries = lax.all_to_all(mention_queries, "head", split_axis=1, concat_axis=0, tiled=True)
    query_row = jnp.concatenate([queries, extra], 1)
    query_x = jnp.stack([query_row] + [shift_x(query_row, d) for d in (1, 2, 3)])

    own = jnp.stack([desc_keys.reshape(OWN, -1), desc_values.reshape(OWN, -1)])
    other = swap(own)
    low_core, high_core = jnp.where(core0, own, other), jnp.where(core0, other, own)
    chip_kv = jnp.concatenate([low_core, high_core], 1)
    first = jnp.where(core0, chip_kv, chip_kv[::-1])
    ring = [first]
    for _ in range(3):
        ring.append(shift_z_apart(ring[-1]))
    far = shift_z_apart(ring[3][0])
    across = [swap(piece) for piece in ring[1:]]
    far_across = swap(far)

    keys = lax.all_to_all(pack_keys, "head", split_axis=1, concat_axis=0, tiled=True)
    values = lax.all_to_all(pack_values, "head", split_axis=1, concat_axis=0, tiled=True)
    positions = mention_positions.reshape(MEN, 1)

    asked = query_x[:, :, COLS : COLS + 6].astype(jnp.int32)
    owner, local, length = [asked[:, :, 2 * i : 2 * i + 2].reshape(NX, LISTED) for i in range(3)]
    match = (owner // (NZ * NC)) == my_x
    entry = jnp.arange(LISTED)
    rank = jnp.sum(match[:, None, :] & (entry[None, None, :] < entry[None, :, None]), 2)
    chosen = match[:, None, :] & (rank[:, None, :] == jnp.arange(SLOTS)[None, :, None])
    away = ((owner // NC) % NZ - my_z) % NZ
    order = jnp.where(
        core0, jnp.array([0, 4, 5, 6, 7, 3, 2, 1], jnp.int32), jnp.array([0, 1, 2, 3, 7, 6, 5, 4], jnp.int32)
    )
    chunk = jnp.sum(jnp.where(away[:, :, None] == jnp.arange(NZ), order, 0), 2)
    row = chunk * CHIP + (owner % NC) * OWN + local * DBLK
    row = jnp.sum(jnp.where(chosen, row[:, None, :], 0), 2)
    half = NZ * CHIP
    row_k = row + jnp.where(core0, 0, half)
    row_v = row + jnp.where(core0, half, 0)
    stretch_of = (entry // (LISTED // 2))[None, None, None, :] == jnp.arange(2)[None, :, None, None]
    live = jnp.sum(jnp.where(chosen[:, None] & stretch_of, length[:, None, None, :], 0), 3)
    bias = jnp.where(jnp.arange(DBLK) < live[..., None], 0.0, LOW).astype(F32).reshape(NX, 2, SPAN)

    shape = jax.ShapeDtypeStruct
    local_part = call(
        self_forward, shape((MEN, WIDE), F32), [queries, keys, values, positions], flops=4 * 10**8, moved=2 * 10**6
    )
    pool = pltpu.VMEM((2 * NZ * CHIP, KV * HEAD_DIM), BF16)
    gathered = shape((NX, SPAN, KV * HEAD_DIM), BF16)
    parts, got_k, got_v = call(
        node_forward,
        (shape((NX, MEN, WIDE), F32), gathered, gathered),
        [row_k, row_v, query_x, bias] + ring + across + [far, far_across],
        smem=(0, 1),
        scratch=[pool],
        flops=10**9,
        moved=10**7,
    )
    returned = [shift_x(parts[d], -d) for d in (1, 2, 3)]
    att, lse, logits = call(
        entity_forward,
        (shape((MEN, COLS), F32), shape((MEN, 128), F32), shape((MEN, 128), F32)),
        [parts[0]] + returned + [local_part, entity_table, teacher_ids],
        flops=10**8,
        moved=3 * 10**6,
    )
    everyone = [logits] + [shift_head(logits, d) for d in (1, 2, 3)]
    teacher = jnp.pad(teacher_logits, ((0, 0), (0, 128 - teacher_logits.shape[1])))
    message, divergence = call(
        entity_backward,
        (shape((MEN, WIDE), BF16), shape((MEN, 128), F32)),
        everyone + [teacher, teacher_ids, entity_table, att, lse],
        flops=3 * 10**8,
        moved=3 * 10**6,
    )
    message_x = jnp.stack([message] + [shift_x(message, d) for d in (1, 2, 3)])

    q_mine = query_x.reshape(NX * MEN, WIDE)
    g_mine = message_x.reshape(NX * MEN, WIDE)
    q_up, q_down, q_far = around_z(q_mine)
    g_up, g_down, g_far = around_z(g_mine)
    chip = (me // NC).reshape(1)
    sums = None
    groups = (
        ([q_mine, q_up[0], q_down[0]], [g_mine, g_up[0], g_down[0]]),
        ([q_up[1], q_down[1]], [g_up[1], g_down[1]]),
        ([q_up[2], q_down[2], *q_far], [g_up[2], g_down[2], *g_far]),
    )
    for qs, gs in groups:
        sums = owner_part(chip, chip_kv[0], chip_kv[1], sums, qs, gs)
    both = jnp.stack(sums).reshape(2, NC, OWN, KV * HEAD_DIM)
    mine = jnp.where(core0, both[:, 0], both[:, 1])
    theirs = jnp.where(core0, both[:, 1], both[:, 0])
    total = mine + swap(theirs)
    my_lengths = lax.dynamic_slice_in_dim(desc_lengths, me * BLK, BLK)
    visible = (jnp.arange(DBLK)[None, :] < my_lengths[:, None])[:, :, None]
    total = total.reshape(2, BLK, DBLK, KV * HEAD_DIM)
    grad_desc_keys = jnp.where(visible, total[0] * SCALE, 0.0)
    grad_desc_values = jnp.where(visible, total[1], 0.0)

    node_q = call(
        node_backward,
        shape((NX, MEN, COLS), BF16),
        [query_x, message_x, bias, got_k, got_v],
        flops=10**9,
        moved=6 * 10**6,
    )
    back_q = [shift_x(node_q[d], -d) for d in (1, 2, 3)]
    pack_shape = shape((2 * STRETCH, KV * HEAD_DIM), BF16)
    local_q, grad_pack_keys, grad_pack_values = call(
        self_backward,
        (shape((MEN, COLS), F32), pack_shape, pack_shape),
        [queries, keys, values, positions, message],
        flops=10**9,
        moved=4 * 10**6,
    )
    grad_queries = functools.reduce(
        jnp.add, [part.astype(F32) for part in [node_q[0]] + back_q], local_q
    ).astype(BF16)
    return (
        grad_queries,
        grad_pack_keys,
        grad_pack_values,
        grad_desc_keys,
        grad_desc_values,
        divergence[:, 0],
    )


def solution(mesh):
    placed = (
        P(("seq", "head"), None),
        P(("seq", "head"), None),
        P(("seq", "head"), None),
        P("seq", None, "head"),
        P("seq", None, "head"),
        P(),
        P("seq", None),
        P(),
        P("seq"),
        P(None, "head"),
        P("seq", None),
        P("seq", None),
    )
    return jax.shard_map(
        per_device,
        mesh=mesh,
        in_specs=placed,
        out_specs=(
            P("seq", "head"),
            P("seq", "head"),
            P("seq", "head"),
            P("seq", None, "head"),
            P("seq", None, "head"),
            P("seq"),
        ),
        check_vma=False,
    )
```

```python
import functools

import jax
import jax.numpy as jnp
from jax import lax
from jax.experimental import pallas as pl
from jax.experimental.pallas import tpu as pltpu
from jax.sharding import Mesh
from jax.sharding import PartitionSpec as P

HEAD_DIM = 128
SCALE = HEAD_DIM ** (-0.5)
NX, NZ, NC, NH = 4, 8, 2, 4
GROUP = 4
KV = 2
HEADS = GROUP * KV
COLS = HEADS * HEAD_DIM
WIDE = COLS + 128
DBLK = 32
BLK = 8
OWN = BLK * DBLK
CHIP = NC * OWN
MEN = 32
MEN_CH = 16
STRETCH = 512
PART = 256
LISTED = 64
SLOTS = 2 * NZ * NC
SPAN = SLOTS * DBLK
LOW = -1e30
F32 = jnp.float32
BF16 = jnp.bfloat16
NT = (((1,), (1,)), ((), ()))
TN = (((0,), (0,)), ((), ()))
VMEM_BYTES = 40 * 1024 * 1024
SEQ = ("x", "z", "core")


def pairs(move):
    out = []
    for x in range(NX):
        for z in range(NZ):
            for c in range(NC):
                tx, tz, tc = move(x, z, c)
                out.append(((x * NZ + z) * NC + c, ((tx % NX) * NZ + tz % NZ) * NC + tc))
    return out


def shift_x(value, step):
    return lax.ppermute(value, SEQ, pairs(lambda x, z, c: (x + step, z, c)))


def shift_z(value, step):
    return lax.ppermute(value, SEQ, pairs(lambda x, z, c: (x, z + step, c)))


def shift_z_apart(value):
    return lax.ppermute(value, SEQ, pairs(lambda x, z, c: (x, z + 1 - 2 * c, c)))


def swap(value):
    return lax.ppermute(value, SEQ, pairs(lambda x, z, c: (x, z, 1 - c)))


def shift_head(value, step):
    return lax.ppermute(value, "head", [(i, (i + step) % NH) for i in range(NH)])


def dot(left, right, dims=(((1,), (0,)), ((), ()))):
    return lax.dot_general(left, right, dims, preferred_element_type=F32)


def head_cols(head):
    return slice(head * HEAD_DIM, (head + 1) * HEAD_DIM)


def call(kernel, out_shape, operands, smem=(), anywhere=(), far_outs=(), scratch=(), flops=0, moved=0):
    space = lambda i: pltpu.SMEM if i in smem else pl.ANY if i in anywhere else pltpu.VMEM
    specs = [pl.BlockSpec(memory_space=space(i)) for i in range(len(operands))]
    outs = [pl.BlockSpec(memory_space=pltpu.HBM if i in far_outs else pltpu.VMEM) for i in range(len(out_shape))]
    return pl.pallas_call(
        kernel,
        out_shape=tuple(out_shape),
        in_specs=specs,
        out_specs=tuple(outs),
        scratch_shapes=list(scratch),
        compiler_params=pltpu.CompilerParams(vmem_limit_bytes=VMEM_BYTES),
        cost_estimate=pl.CostEstimate(flops=flops, bytes_accessed=moved, transcendentals=0),
    )(*operands)


def stack_heads(ref, kv, rows):
    return jnp.concatenate([ref[rows, head_cols(kv * GROUP + g)] for g in range(GROUP)], 0)


def stack_numbers(tile, kv):
    return jnp.concatenate([tile[:, kv * GROUP + g : kv * GROUP + g + 1] for g in range(GROUP)], 0)


def unpack_numbers(tile):
    first = tile + pltpu.roll(tile, 120, 1) + pltpu.roll(tile, 112, 1)
    second = pltpu.roll(tile, 104, 1) + pltpu.roll(tile, 96, 1) + pltpu.roll(tile, 88, 1)
    return first, second


def three_parts(value):
    high = value.astype(BF16).astype(F32)
    rest = value - high
    middle = rest.astype(BF16).astype(F32)
    return high, middle, (rest - middle).astype(BF16).astype(F32)


def attend(scores, values):
    top = jnp.max(scores, axis=1, keepdims=True)
    weights = jnp.exp(scores - top)
    total = jnp.sum(weights, axis=1, keepdims=True)
    return dot(weights.astype(BF16), values) / total, top + jnp.log(total)


def own_rows(ref, t, which, kv):
    span = slice(which * PART, (which + 1) * PART)
    return jnp.concatenate([ref[2 * t, span, head_cols(kv)], ref[2 * t + 1, span, head_cols(kv)]], 0)


def self_forward(queries, pack, positions, out):
    lane = lax.broadcasted_iota(jnp.int32, (MEN_CH, 128), 1)
    token = lax.broadcasted_iota(jnp.int32, (GROUP * MEN_CH, STRETCH), 1)
    for t in range(2):
        rows = slice(t * MEN_CH, (t + 1) * MEN_CH)
        place = jnp.concatenate([positions[rows, :]] * GROUP, 0)
        tile = jnp.zeros((MEN_CH, 128), F32)
        for kv in range(KV):
            q = stack_heads(queries, kv, rows)
            scores = dot(q, own_rows(pack, t, 0, kv), NT) * SCALE
            scores = jnp.where(token <= place, scores, LOW)
            att, lse = attend(scores, own_rows(pack, t, 1, kv))
            for g in range(GROUP):
                head = kv * GROUP + g
                part = slice(g * MEN_CH, (g + 1) * MEN_CH)
                out[rows, head_cols(head)] = att[part]
                tile = jnp.where(lane == head, lse[part], tile)
        out[rows, COLS:WIDE] = tile


def self_backward(queries, pack, positions, message, out_q, out_k, out_v):
    token = lax.broadcasted_iota(jnp.int32, (GROUP * MEN_CH, STRETCH), 1)
    for t in range(2):
        rows = slice(t * MEN_CH, (t + 1) * MEN_CH)
        span = slice(t * STRETCH, (t + 1) * STRETCH)
        place = jnp.concatenate([positions[rows, :]] * GROUP, 0)
        lse, center = unpack_numbers(message[rows, COLS:WIDE].astype(F32))
        for kv in range(KV):
            q = stack_heads(queries, kv, rows)
            grad = stack_heads(message, kv, rows)
            key = own_rows(pack, t, 0, kv)
            value = own_rows(pack, t, 1, kv)
            scores = dot(q, key, NT) * SCALE
            scores = jnp.where(token <= place, scores, LOW)
            probs = jnp.exp(scores - stack_numbers(lse, kv))
            grad_scores = probs * (dot(grad, value, NT) - stack_numbers(center, kv))
            low = grad_scores.astype(BF16)
            grad_q = dot(low, key) * SCALE
            for g in range(GROUP):
                out_q[rows, head_cols(kv * GROUP + g)] = grad_q[g * MEN_CH : (g + 1) * MEN_CH]
            out_k[span, head_cols(kv)] = (dot(low, q, TN) * SCALE).astype(BF16)
            out_v[span, head_cols(kv)] = dot(probs.astype(BF16), grad, TN).astype(BF16)


def masked(scores, bias):
    four = scores.reshape(GROUP, 2, MEN_CH, SPAN) + bias[None, :, None, :]
    return four.reshape(GROUP * MEN, SPAN)


def slot_kernel(order, place, q0, q1, q2, q3, out_rows, out_bias):
    lane = lax.broadcasted_iota(jnp.int32, (2, 128), 1)
    before = lax.broadcasted_iota(jnp.int32, (128, 128), 0) < lax.broadcasted_iota(jnp.int32, (128, 128), 1)
    before = jnp.where(before, 1.0, 0.0).astype(BF16)
    slot = lax.broadcasted_iota(jnp.int32, (SLOTS, 128), 0)
    wide = lax.broadcasted_iota(jnp.int32, (SLOTS, 128), 1)
    spread = lax.broadcasted_iota(jnp.int32, (SLOTS, SPAN), 1) // DBLK
    spread = spread == lax.broadcasted_iota(jnp.int32, (SLOTS, SPAN), 0)
    spread = jnp.where(spread, 1.0, 0.0).astype(BF16)
    row_in = (lax.broadcasted_iota(jnp.int32, (1, SPAN), 1) % DBLK).astype(F32)
    rows = jnp.zeros((SLOTS, 128), jnp.int32)
    for r, queries in enumerate((q0, q1, q2, q3)):
        tile = queries[0:16, COLS:WIDE]
        numbers = tile.astype(F32).astype(jnp.int32)
        owner, local = numbers[0:2], numbers[2:4]
        match = (owner // (NZ * NC) == place[0]) & (lane < LISTED // 2)
        ones = jnp.where(match, 1.0, 0.0)
        rank = dot(ones.astype(BF16), before)
        first = jnp.sum(ones[0:1], axis=1, keepdims=True)
        rank = jnp.concatenate([rank[0:1], rank[1:2] + first], 0).astype(jnp.int32)
        away = ((owner // NC) % NZ + (NZ - place[1])) % NZ
        chunk = jnp.zeros_like(away)
        for i in range(NZ):
            chunk = jnp.where(away == i, order[i], chunk)
        row = chunk * CHIP + (owner % NC) * OWN + local * DBLK
        column = jnp.zeros((SLOTS, 1), jnp.int32)
        for t in range(2):
            chosen = (slot == rank[t : t + 1]) & (ones[t : t + 1] > 0.5)
            column = column + jnp.sum(jnp.where(chosen, row[t : t + 1], 0), axis=1, keepdims=True)
            live = dot(tile, jnp.where(chosen, 1.0, 0.0).astype(BF16), NT)
            live = dot(live.astype(BF16), spread)[4 + t : 5 + t]
            out_bias[r, t : t + 1, :] = jnp.where(row_in < live, 0.0, LOW)
        rows = jnp.where(wide == r, column, rows)
    out_rows[...] = rows


def node_forward(base, row, q0, q1, q2, q3, bias, *refs):
    ring, across, far, far_across = refs[:4], refs[4:7], refs[7], refs[8]
    outs, out_k, out_v, pool, kept_k, kept_v, sems_in, sems_out = refs[9:13], *refs[13:]
    half = NZ * CHIP
    pieces = [(piece.at[0], i) for i, piece in enumerate(ring)]
    pieces += [(piece.at[1], NZ + i) for i, piece in enumerate(ring)]
    pieces += [(piece.at[1], 4 + i) for i, piece in enumerate(across)]
    pieces += [(piece.at[0], NZ + 4 + i) for i, piece in enumerate(across)]
    pieces += [(far, 7), (far_across, NZ + 7)]
    copies = [
        pltpu.make_async_copy(piece, pool.at[pl.ds(i * CHIP, CHIP), :], sems_in.at[n])
        for n, (piece, i) in enumerate(pieces)
    ]
    for copy in copies:
        copy.start()
    for copy in copies:
        copy.wait()
    lane = lax.broadcasted_iota(jnp.int32, (MEN, 128), 1)
    copies = []
    for r, (queries, out) in enumerate(zip((q0, q1, q2, q3), outs)):
        for j in range(SLOTS):
            rows = slice(j * DBLK, (j + 1) * DBLK)
            kept_k[r, rows, :] = pool[pl.ds(pl.multiple_of(base[0] + row[j, r], DBLK), DBLK), :]
            kept_v[r, rows, :] = pool[pl.ds(pl.multiple_of(base[1] + row[j, r], DBLK), DBLK), :]
        copies.append(pltpu.make_async_copy(kept_k.at[r], out_k.at[r], sems_out.at[2 * r]))
        copies.append(pltpu.make_async_copy(kept_v.at[r], out_v.at[r], sems_out.at[2 * r + 1]))
        copies[-2].start()
        copies[-1].start()
        tile = jnp.zeros((MEN, 128), F32)
        for kv in range(KV):
            q = stack_heads(queries, kv, slice(None))
            scores = masked(dot(q, kept_k[r, :, head_cols(kv)], NT) * SCALE, bias[r])
            att, lse = attend(scores, kept_v[r, :, head_cols(kv)])
            for g in range(GROUP):
                head = kv * GROUP + g
                part = slice(g * MEN, (g + 1) * MEN)
                out[:, head_cols(head)] = att[part]
                tile = jnp.where(lane == head, lse[part], tile)
        out[:, COLS:WIDE] = tile
    for copy in copies:
        copy.wait()


def node_backward(q0, q1, q2, q3, g0, g1, g2, g3, bias, keys, values, *outs):
    for r, (queries, message, out) in enumerate(zip((q0, q1, q2, q3), (g0, g1, g2, g3), outs)):
        lse, center = unpack_numbers(message[:, COLS:WIDE].astype(F32))
        for kv in range(KV):
            q = stack_heads(queries, kv, slice(None))
            grad = stack_heads(message, kv, slice(None))
            key = keys[r, :, head_cols(kv)]
            scores = masked(dot(q, key, NT) * SCALE, bias[r])
            probs = jnp.exp(scores - stack_numbers(lse, kv))
            grad_probs = dot(grad, values[r, :, head_cols(kv)], NT)
            low = (probs * (grad_probs - stack_numbers(center, kv))).astype(BF16)
            grad_q = (dot(low, key) * SCALE).astype(BF16)
            for g in range(GROUP):
                out[:, head_cols(kv * GROUP + g)] = grad_q[g * MEN : (g + 1) * MEN]


def entity_forward(own, y1, y2, y3, local, table, ids, out_att, out_lse, out_logits):
    parts = (own, y1, y2, y3, local)
    lses = [part[:, COLS:WIDE] for part in parts]
    top = functools.reduce(jnp.maximum, lses)
    weights = [jnp.exp(lse - top) for lse in lses]
    total = functools.reduce(jnp.add, weights)
    out_lse[...] = top + jnp.log(total)
    weights = [weight / total for weight in weights]
    lows = []
    for head in range(HEADS):
        att = functools.reduce(
            jnp.add, [part[:, head_cols(head)] * w[:, head : head + 1] for part, w in zip(parts, weights)]
        )
        out_att[:, head_cols(head)] = att
        lows.append(att.astype(BF16))
    every = dot(jnp.concatenate(lows, 1), table[...], NT)
    entity = lax.broadcasted_iota(jnp.int32, every.shape, 1)
    lane = lax.broadcasted_iota(jnp.int32, (MEN, 128), 1)
    logits = jnp.zeros((MEN, 128), F32)
    for k in range(ids.shape[1]):
        picked = jnp.sum(jnp.where(entity == ids[:, k : k + 1], every, 0.0), axis=1, keepdims=True)
        logits = jnp.where(lane == k, picked, logits)
    out_logits[...] = logits


def log_softmax(values, live):
    values = jnp.where(live, values, LOW)
    values = values - jnp.max(values, axis=1, keepdims=True)
    return values - jnp.log(jnp.sum(jnp.exp(values), axis=1, keepdims=True))


def entity_backward(l0, l1, l2, l3, teacher, ids, table, att, lse, out, out_div):
    count = ids.shape[1]
    lane = lax.broadcasted_iota(jnp.int32, (MEN, 128), 1)
    live = lane < count
    log_model = log_softmax((l0[...] + l2[...]) + (l1[...] + l3[...]), live)
    log_target = log_softmax(teacher[...], live)
    target = jnp.where(live, jnp.exp(log_target), 0.0)
    terms = jnp.where(live, target * (log_target - log_model), 0.0)
    out_div[...] = jnp.broadcast_to(jnp.sum(terms, axis=1, keepdims=True), (MEN, 128))
    grad_logits = jnp.where(live, jnp.exp(log_model), 0.0) - target
    entity = lax.broadcasted_iota(jnp.int32, (MEN, table.shape[0]), 1)
    spread = jnp.zeros((MEN, table.shape[0]), F32)
    for k in range(count):
        spread = jnp.where(entity == ids[:, k : k + 1], grad_logits[:, k : k + 1], spread)
    high, middle, low = three_parts(spread)
    three = dot(jnp.concatenate([high, middle, low], 0).astype(BF16), table[...])
    grad = (three[:MEN] + three[MEN : 2 * MEN] + three[2 * MEN :]).astype(BF16)
    out[:, :COLS] = grad
    center = jnp.zeros((MEN, 128), F32)
    for head in range(HEADS):
        product = grad[:, head_cols(head)].astype(F32) * att[:, head_cols(head)]
        center = jnp.where(lane == head, jnp.sum(product, axis=1, keepdims=True), center)
    numbers = jnp.zeros((MEN, 128), F32)
    for i, part in enumerate(three_parts(jnp.where(lane < HEADS, lse[...], 0.0)) + three_parts(center)):
        numbers = numbers + (pltpu.roll(part, i * HEADS, 1) if i else part)
    out[:, COLS:WIDE] = numbers.astype(BF16)


def owner_kernel(count, has_start, chip, keys, values, *refs):
    refs = list(refs)
    start = (refs.pop(0), refs.pop(0)) if has_start else None
    qs = [refs.pop(0) for _ in range(count)]
    gs = [refs.pop(0) for _ in range(count)]
    out_k, out_v, q_all, g_all = refs
    at = 0
    for q, g in zip(qs, gs):
        q_all[at : at + q.shape[0], :] = q[...]
        g_all[at : at + g.shape[0], :] = g[...]
        at += g.shape[0]
    if start is None:
        out_k[...] = jnp.zeros_like(out_k)
        out_v[...] = jnp.zeros_like(out_v)
    else:
        out_k[...] = start[0][...]
        out_v[...] = start[1][...]
    blocks = CHIP // DBLK
    base = chip[0] * blocks
    block = lax.broadcasted_iota(jnp.int32, (blocks, 128), 0) + base
    group = lax.broadcasted_iota(jnp.int32, (blocks, 128), 1) // MEN_CH

    def step(i, carry):
        rows = pl.ds(pl.multiple_of(i * 128, 128), 128)
        listed = jnp.zeros((blocks, 128), F32)
        for r in range(NX):
            tile = q_all[pl.ds(pl.multiple_of(i * 128 + r * MEN, MEN), 16), COLS:WIDE].astype(F32)
            stored = (tile[0:2] * BLK + tile[2:4]).astype(jnp.int32)
            for t in range(2):
                hit = jnp.where(stored[t : t + 1] == block, 1.0, 0.0)
                hit = jnp.max(hit, axis=1, keepdims=True)
                listed = jnp.where(group == 2 * r + t, hit, listed)
        numbers = jnp.transpose(g_all[rows, COLS:WIDE].astype(F32))
        lse = numbers[0:8] + numbers[8:16] + numbers[16:24]
        center = numbers[24:32] + numbers[32:40] + numbers[40:48]
        for kv in range(KV):
            heads = range(kv * GROUP, (kv + 1) * GROUP)
            q = jnp.concatenate([q_all[rows, head_cols(h)] for h in heads], 0)
            g = jnp.concatenate([g_all[rows, head_cols(h)] for h in heads], 0)
            offset = jnp.concatenate([jnp.where(listed > 0.5, -lse[h : h + 1], LOW) for h in heads], 1)
            middle = jnp.concatenate([center[h : h + 1] for h in heads], 1)
            scores = dot(keys[:, head_cols(kv)], q, NT) * SCALE
            scores = scores.reshape(blocks, DBLK, scores.shape[1]) + offset[:, None, :]
            probs = jnp.exp(scores.reshape(CHIP, scores.shape[2]))
            grad_probs = dot(values[:, head_cols(kv)], g, NT)
            low = (probs * (grad_probs - middle)).astype(BF16)
            out_v[:, head_cols(kv)] += dot(probs.astype(BF16), g)
            out_k[:, head_cols(kv)] += dot(low, q)
        return carry

    lax.fori_loop(0, at // 128, step, 0)


def owner_part(chip, keys, values, start, qs, gs):
    shape = jax.ShapeDtypeStruct((CHIP, KV * HEAD_DIM), F32)
    rows = sum(q.shape[0] for q in qs)
    operands = [chip, keys, values] + list(start or ()) + list(qs) + list(gs)
    return call(
        functools.partial(owner_kernel, len(qs), start is not None),
        (shape, shape),
        operands,
        smem=(0,),
        scratch=[pltpu.VMEM((rows, WIDE), BF16), pltpu.VMEM((rows, WIDE), BF16)],
        flops=8 * rows * HEADS * CHIP * HEAD_DIM,
        moved=4 * rows * WIDE + 12 * CHIP * KV * HEAD_DIM,
    )


def both_ways(up, down):
    return shift_z(up, 1), shift_z(down, -1)


def last_way(up, down):
    half = up.shape[0] // 2
    return shift_z(up[:half], 1), shift_z(down[half:], -1)


def per_device(
    mention_queries,
    pack_keys,
    pack_values,
    desc_keys,
    desc_values,
    desc_lengths,
    block_lists,
    block_home,
    mention_positions,
    entity_table,
    teacher_ids,
    teacher_logits,
):
    my_x, my_z, my_c = (lax.axis_index(name) for name in SEQ)
    chip = my_x * NZ + my_z
    me = chip * NC + my_c
    core0 = my_c == 0
    shape = jax.ShapeDtypeStruct
    hold = lax.optimization_barrier

    own = jnp.stack([desc_keys.reshape(OWN, -1), desc_values.reshape(OWN, -1)])
    other = swap(own)
    low_core, high_core = jnp.where(core0, own, other), jnp.where(core0, other, own)
    chip_kv = jnp.concatenate([low_core, high_core], 1)
    first = jnp.where(core0, chip_kv, chip_kv[::-1])
    ring = [first, shift_z_apart(first)]

    home = jnp.take(block_home, block_lists)
    lengths = jnp.take(desc_lengths, home)
    extra = jnp.pad(jnp.concatenate([home // BLK, home % BLK, lengths], 0), ((0, 0), (0, 128 - LISTED // 2)), constant_values=255)
    extra = jnp.pad(extra, ((0, MEN - extra.shape[0]), (0, 0))).astype(BF16)
    positions = mention_positions.reshape(MEN, 1)
    teacher = jnp.pad(teacher_logits, ((0, 0), (0, 128 - teacher_logits.shape[1])))
    ring[1], extra, positions, teacher, teacher_ids, mention_queries = hold(
        (ring[1], extra, positions, teacher, teacher_ids, mention_queries)
    )
    ring.append(shift_z_apart(ring[1]))
    queries = lax.all_to_all(mention_queries, "head", split_axis=1, concat_axis=0, tiled=True)
    query_row = jnp.concatenate([queries, extra], 1)
    q = [query_row] + [shift_x(query_row, d) for d in (1, 2, 3)]

    pack = jnp.concatenate(
        [rows.reshape(PART, NH, KV * HEAD_DIM).transpose(1, 0, 2) for rows in (pack_keys, pack_values)], 1
    )
    ring[2], pack = hold((ring[2], pack))
    ring.append(shift_z_apart(ring[2]))
    pack = lax.all_to_all(pack, "head", split_axis=0, concat_axis=0, tiled=True)
    (local_part,) = call(
        self_forward, [shape((MEN, WIDE), F32)], [queries, pack, positions], flops=10**9, moved=2 * 10**6
    )
    order = jnp.where(
        core0, jnp.array([0, 4, 5, 6, 7, 3, 2, 1], jnp.int32), jnp.array([0, 1, 2, 3, 7, 6, 5, 4], jnp.int32)
    )
    row, bias = call(
        slot_kernel,
        [shape((SLOTS, 128), jnp.int32), shape((NX, 2, SPAN), F32)],
        [order, jnp.stack([my_x, my_z])] + q,
        smem=(0, 1),
        flops=10**9,
        moved=10**5,
    )
    q_mine = jnp.concatenate(q, 0)
    far = shift_z_apart(ring[3][0])
    across = [swap(piece) for piece in ring[1:]]
    far, local_part, row, bias, q_mine, across = hold((far, local_part, row, bias, q_mine, across))
    far_across = swap(far)
    q_ring = [both_ways(q_mine, q_mine)]

    base = jnp.where(core0, jnp.array([0, NZ * CHIP], jnp.int32), jnp.array([NZ * CHIP, 0], jnp.int32))
    gathered = shape((NX, SPAN, KV * HEAD_DIM), BF16)
    kept = pltpu.VMEM(gathered.shape, BF16)
    *parts, got_k, got_v = call(
        node_forward,
        [shape((MEN, WIDE), F32)] * NX + [gathered, gathered],
        [base, row] + q + [bias] + ring + across + [far, far_across],
        smem=(0, 1),
        anywhere=range(7, 16),
        far_outs=(4, 5),
        scratch=[
            pltpu.VMEM((2 * NZ * CHIP, KV * HEAD_DIM), BF16),
            kept,
            kept,
            pltpu.SemaphoreType.DMA((2 * NZ,)),
            pltpu.SemaphoreType.DMA((2 * NX,)),
        ],
        flops=10**9,
        moved=10**7,
    )
    parts, q_ring[0] = hold((parts, q_ring[0]))
    returned = [shift_x(parts[d], -d) for d in (1, 2, 3)]
    q_ring.append(both_ways(*q_ring[0]))
    returned, q_ring[1] = hold((returned, q_ring[1]))
    att, lse, logits = call(
        entity_forward,
        [shape((MEN, COLS), F32), shape((MEN, 128), F32), shape((MEN, 128), F32)],
        [parts[0]] + returned + [local_part, entity_table, teacher_ids],
        flops=10**8,
        moved=3 * 10**6,
    )
    everyone = [logits] + [shift_head(logits, d) for d in (1, 2, 3)]
    q_ring.append(both_ways(*q_ring[1]))
    message, divergence = call(
        entity_backward,
        [shape((MEN, WIDE), BF16), shape((MEN, 128), F32)],
        everyone + [teacher, teacher_ids, entity_table, att, lse],
        flops=3 * 10**8,
        moved=3 * 10**6,
    )
    message, q_ring[2] = hold((message, q_ring[2]))
    g = [message] + [shift_x(message, d) for d in (1, 2, 3)]

    pack_shape = shape((2 * STRETCH, KV * HEAD_DIM), BF16)
    local_q, grad_pack_keys, grad_pack_values = call(
        self_backward,
        [shape((MEN, COLS), F32), pack_shape, pack_shape],
        [queries, pack, positions, message],
        flops=10**9,
        moved=4 * 10**6,
    )
    q_ring.append(last_way(*q_ring[2]))
    g, local_q, q_ring[3] = hold((g, local_q, q_ring[3]))

    def owner(start, qs, gs):
        return owner_part(chip.reshape(1), chip_kv[0], chip_kv[1], start, qs, gs)

    g_mine = jnp.concatenate(g, 0)
    g_ring = [both_ways(g_mine, g_mine)]
    node_q = call(
        node_backward,
        [shape((MEN, COLS), BF16)] * NX,
        q + g + [bias, got_k, got_v],
        flops=10**9,
        moved=6 * 10**6,
    )
    sums = owner(None, [q_mine], [g_mine])
    g_ring[0], node_q = hold((g_ring[0], node_q))
    back_q = [shift_x(node_q[d], -d) for d in (1, 2, 3)]
    g_ring.append(both_ways(*g_ring[0]))
    sums = owner(sums, q_ring[0], g_ring[0])
    g_ring[1], sums = hold((g_ring[1], sums))
    g_ring.append(both_ways(*g_ring[1]))
    sums = owner(sums, q_ring[1], g_ring[1])
    g_ring[2], sums, back_q = hold((g_ring[2], sums, back_q))
    g_ring.append(last_way(*g_ring[2]))
    sums = owner(sums, q_ring[2], g_ring[2])
    grad_queries = functools.reduce(
        jnp.add, [part.astype(F32) for part in [node_q[0]] + back_q], local_q
    ).astype(BF16)
    g_ring[3], sums, grad_queries, divergence = hold((g_ring[3], sums, grad_queries, divergence[:, 0]))
    sums = owner(sums, q_ring[3], g_ring[3])
    both = jnp.stack(sums).reshape(2, NC, OWN, KV * HEAD_DIM)
    mine = jnp.where(core0, both[:, 0], both[:, 1])
    theirs = jnp.where(core0, both[:, 1], both[:, 0])
    total = mine + swap(theirs.astype(BF16)).astype(F32)
    my_lengths = lax.dynamic_slice_in_dim(desc_lengths, me * BLK, BLK)
    visible = (jnp.arange(DBLK)[None, :] < my_lengths[:, None])[:, :, None]
    total = total.reshape(2, BLK, DBLK, KV * HEAD_DIM)
    grad_desc_keys = jnp.where(visible, total[0] * SCALE, 0.0)
    grad_desc_values = jnp.where(visible, total[1], 0.0)
    return (
        grad_queries,
        grad_pack_keys,
        grad_pack_values,
        grad_desc_keys,
        grad_desc_values,
        divergence,
    )


def solution(mesh):
    axes = Mesh(mesh.devices.reshape(NX, NZ, NC, NH), SEQ + ("head",))
    placed = (
        P(SEQ + ("head",), None),
        P(SEQ + ("head",), None),
        P(SEQ + ("head",), None),
        P(SEQ, None, "head"),
        P(SEQ, None, "head"),
        P(),
        P(SEQ, None),
        P(),
        P(SEQ),
        P(None, "head"),
        P(SEQ, None),
        P(SEQ, None),
    )
    return jax.shard_map(
        per_device,
        mesh=axes,
        in_specs=placed,
        out_specs=(
            P(SEQ, "head"),
            P(SEQ, "head"),
            P(SEQ, "head"),
            P(SEQ, None, "head"),
            P(SEQ, None, "head"),
            P(SEQ),
        ),
        check_vma=False,
    )
```

```python
import functools

import jax
import jax.numpy as jnp
from jax import lax
from jax.experimental import pallas as pl
from jax.experimental.pallas import tpu as pltpu
from jax.sharding import Mesh
from jax.sharding import PartitionSpec as P

HEAD_DIM = 128
SCALE = HEAD_DIM ** (-0.5)
NX, NZ, NC, NH = 4, 8, 2, 4
GROUP = 4
KV = 2
HEADS = GROUP * KV
COLS = HEADS * HEAD_DIM
WIDE = COLS + 128
DBLK = 32
BLK = 8
OWN = BLK * DBLK
CHIP = NC * OWN
MEN = 32
MEN_CH = 16
STRETCH = 512
PART = 256
LISTED = 64
TOPK = 16
SLOTS = 2 * NZ * NC
SPAN = SLOTS * DBLK
LOW = -1e30
F32 = jnp.float32
BF16 = jnp.bfloat16
NT = (((1,), (1,)), ((), ()))
TN = (((0,), (0,)), ((), ()))
VMEM_BYTES = 40 * 1024 * 1024
SEQ = ("x", "z", "core")


def pairs(move):
    out = []
    for x in range(NX):
        for z in range(NZ):
            for c in range(NC):
                tx, tz, tc = move(x, z, c)
                out.append(((x * NZ + z) * NC + c, ((tx % NX) * NZ + tz % NZ) * NC + tc))
    return out


def shift_x(value, step):
    return lax.ppermute(value, SEQ, pairs(lambda x, z, c: (x + step, z, c)))


def shift_z(value, step):
    return lax.ppermute(value, SEQ, pairs(lambda x, z, c: (x, z + step, c)))


def swap(value):
    return lax.ppermute(value, SEQ, pairs(lambda x, z, c: (x, z, 1 - c)))


def shift_head(value, step):
    return lax.ppermute(value, "head", [(i, (i + step) % NH) for i in range(NH)])


def dot(left, right, dims=(((1,), (0,)), ((), ()))):
    return lax.dot_general(left, right, dims, preferred_element_type=F32)


def head_cols(head):
    return slice(head * HEAD_DIM, (head + 1) * HEAD_DIM)


def call(kernel, out_shape, operands, smem=(), anywhere=(), far_outs=(), scratch=(), flops=0, moved=0, vmem=VMEM_BYTES):
    space = lambda i: pltpu.SMEM if i in smem else pl.ANY if i in anywhere else pltpu.VMEM
    specs = [pl.BlockSpec(memory_space=space(i)) for i in range(len(operands))]
    outs = [pl.BlockSpec(memory_space=pltpu.HBM if i in far_outs else pltpu.VMEM) for i in range(len(out_shape))]
    return pl.pallas_call(
        kernel,
        out_shape=tuple(out_shape),
        in_specs=specs,
        out_specs=tuple(outs),
        scratch_shapes=list(scratch),
        compiler_params=pltpu.CompilerParams(vmem_limit_bytes=vmem),
        cost_estimate=pl.CostEstimate(flops=flops, bytes_accessed=moved, transcendentals=0),
    )(*operands)


def stack_heads(ref, kv, rows):
    return jnp.concatenate([ref[rows, head_cols(kv * GROUP + g)] for g in range(GROUP)], 0)


def stack_numbers(tile, kv):
    return jnp.concatenate([tile[:, kv * GROUP + g : kv * GROUP + g + 1] for g in range(GROUP)], 0)


def unpack_numbers(tile):
    first = tile + pltpu.roll(tile, 120, 1) + pltpu.roll(tile, 112, 1)
    second = pltpu.roll(tile, 104, 1) + pltpu.roll(tile, 96, 1) + pltpu.roll(tile, 88, 1)
    return first, second


def three_parts(value):
    high = value.astype(BF16).astype(F32)
    rest = value - high
    middle = rest.astype(BF16).astype(F32)
    return high, middle, (rest - middle).astype(BF16).astype(F32)


def attend(scores, values):
    top = jnp.max(scores, axis=1, keepdims=True)
    weights = jnp.exp(scores - top)
    total = jnp.sum(weights, axis=1, keepdims=True)
    return dot(weights.astype(BF16), values) / total, top + jnp.log(total)


def pack_kernel(keys, values, out):
    for h in range(NH):
        cols = slice(h * KV * HEAD_DIM, (h + 1) * KV * HEAD_DIM)
        out[h, :PART, :] = keys[:, cols]
        out[h, PART:, :] = values[:, cols]


def own_rows(ref, t, which, kv):
    span = slice(which * PART, (which + 1) * PART)
    return jnp.concatenate([ref[2 * t, span, head_cols(kv)], ref[2 * t + 1, span, head_cols(kv)]], 0)


def self_forward(queries, pack, positions, out):
    lane = lax.broadcasted_iota(jnp.int32, (MEN_CH, 128), 1)
    token = lax.broadcasted_iota(jnp.int32, (GROUP * MEN_CH, STRETCH), 1)
    for t in range(2):
        rows = slice(t * MEN_CH, (t + 1) * MEN_CH)
        place = jnp.concatenate([positions[rows, :]] * GROUP, 0)
        tile = jnp.zeros((MEN_CH, 128), F32)
        for kv in range(KV):
            q = stack_heads(queries, kv, rows)
            scores = dot(q, own_rows(pack, t, 0, kv), NT) * SCALE
            scores = jnp.where(token <= place, scores, LOW)
            att, lse = attend(scores, own_rows(pack, t, 1, kv))
            for g in range(GROUP):
                head = kv * GROUP + g
                part = slice(g * MEN_CH, (g + 1) * MEN_CH)
                out[rows, head_cols(head)] = att[part]
                tile = jnp.where(lane == head, lse[part], tile)
        out[rows, COLS:WIDE] = tile


def self_backward(queries, pack, positions, message, out_q, out_k, out_v):
    token = lax.broadcasted_iota(jnp.int32, (GROUP * MEN_CH, STRETCH), 1)
    for t in range(2):
        rows = slice(t * MEN_CH, (t + 1) * MEN_CH)
        span = slice(t * STRETCH, (t + 1) * STRETCH)
        place = jnp.concatenate([positions[rows, :]] * GROUP, 0)
        lse, center = unpack_numbers(message[rows, COLS:WIDE].astype(F32))
        for kv in range(KV):
            q = stack_heads(queries, kv, rows)
            grad = stack_heads(message, kv, rows)
            key = own_rows(pack, t, 0, kv)
            value = own_rows(pack, t, 1, kv)
            scores = dot(q, key, NT) * SCALE
            scores = jnp.where(token <= place, scores, LOW)
            probs = jnp.exp(scores - stack_numbers(lse, kv))
            grad_scores = probs * (dot(grad, value, NT) - stack_numbers(center, kv))
            low = grad_scores.astype(BF16)
            grad_q = dot(low, key) * SCALE
            for g in range(GROUP):
                out_q[rows, head_cols(kv * GROUP + g)] = grad_q[g * MEN_CH : (g + 1) * MEN_CH]
            out_k[span, head_cols(kv)] = (dot(low, q, TN) * SCALE).astype(BF16)
            out_v[span, head_cols(kv)] = dot(probs.astype(BF16), grad, TN).astype(BF16)


def masked(scores, bias):
    four = scores.reshape(GROUP, 2, MEN_CH, SPAN) + bias[None, :, None, :]
    return four.reshape(GROUP * MEN, SPAN)


def slot_kernel(place, q0, q1, q2, q3, out_rows, out_bias):
    lane = lax.broadcasted_iota(jnp.int32, (2, 128), 1)
    before = lax.broadcasted_iota(jnp.int32, (128, 128), 0) < lax.broadcasted_iota(jnp.int32, (128, 128), 1)
    before = jnp.where(before, 1.0, 0.0).astype(BF16)
    slot = lax.broadcasted_iota(jnp.int32, (SLOTS, 128), 0)
    wide = lax.broadcasted_iota(jnp.int32, (SLOTS, 128), 1)
    spread = lax.broadcasted_iota(jnp.int32, (SLOTS, SPAN), 1) // DBLK
    spread = spread == lax.broadcasted_iota(jnp.int32, (SLOTS, SPAN), 0)
    spread = jnp.where(spread, 1.0, 0.0).astype(BF16)
    row_in = (lax.broadcasted_iota(jnp.int32, (1, SPAN), 1) % DBLK).astype(F32)
    rows = jnp.zeros((SLOTS, 128), jnp.int32)
    for r, queries in enumerate((q0, q1, q2, q3)):
        tile = queries[0:16, COLS:WIDE]
        numbers = tile.astype(F32).astype(jnp.int32)
        owner, local = numbers[0:2], numbers[2:4]
        match = (owner // (NZ * NC) == place[0]) & (lane < LISTED // 2)
        ones = jnp.where(match, 1.0, 0.0)
        rank = dot(ones.astype(BF16), before)
        first = jnp.sum(ones[0:1], axis=1, keepdims=True)
        rank = jnp.concatenate([rank[0:1], rank[1:2] + first], 0).astype(jnp.int32)
        away = ((owner // NC) % NZ + (NZ - place[1])) % NZ
        row = away * CHIP + ((owner + place[2]) % NC) * OWN + local * DBLK
        column = jnp.zeros((SLOTS, 1), jnp.int32)
        for t in range(2):
            chosen = (slot == rank[t : t + 1]) & (ones[t : t + 1] > 0.5)
            column = column + jnp.sum(jnp.where(chosen, row[t : t + 1], 0), axis=1, keepdims=True)
            live = dot(tile, jnp.where(chosen, 1.0, 0.0).astype(BF16), NT)
            live = dot(live.astype(BF16), spread)[4 + t : 5 + t]
            out_bias[r, t : t + 1, :] = jnp.where(row_in < live, 0.0, LOW)
        rows = jnp.where(wide == r, column, rows)
    out_rows[...] = rows


def node_forward(row, q0, q1, q2, q3, bias, *refs):
    near, far = refs[:14], refs[14:18]
    outs, out_k, out_v, pool, kept_k, kept_v, q_all, out_all, sems_in, sems_out = refs[18:22], *refs[22:]
    half = NZ * CHIP
    pieces = []
    for i, piece in enumerate(near):
        away, other = ((0, 7, 6, 5, 1, 2, 3)[i // 2], i % 2)
        pieces += [(piece.at[0], 2 * away + other), (piece.at[1], 2 * (NZ + away) + other)]
    pieces += [(far[0], 8), (far[1], 9), (far[2], 2 * NZ + 8), (far[3], 2 * NZ + 9)]
    copies = [
        pltpu.make_async_copy(piece, pool.at[pl.ds(i * OWN, OWN), :], sems_in.at[i]) for piece, i in pieces
    ]
    for copy in copies:
        copy.start()
    for copy in copies:
        copy.wait()
    for r, queries in enumerate((q0, q1, q2, q3)):
        q_all[r] = queries[...]
    lane = lax.broadcasted_iota(jnp.int32, (MEN, 128), 1)

    def kept_copies(r):
        return (
            pltpu.make_async_copy(kept_k.at[r], out_k.at[r], sems_out.at[2 * r]),
            pltpu.make_async_copy(kept_v.at[r], out_v.at[r], sems_out.at[2 * r + 1]),
        )

    def step(r, carry):
        for j in range(SLOTS):
            rows = slice(j * DBLK, (j + 1) * DBLK)
            kept_k[r, rows, :] = pool[pl.ds(pl.multiple_of(row[j, r], DBLK), DBLK), :]
            kept_v[r, rows, :] = pool[pl.ds(pl.multiple_of(half + row[j, r], DBLK), DBLK), :]
        for copy in kept_copies(r):
            copy.start()
        tile = jnp.zeros((MEN, 128), F32)
        for kv in range(KV):
            q = stack_heads(q_all.at[r], kv, slice(None))
            scores = masked(dot(q, kept_k[r, :, head_cols(kv)], NT) * SCALE, bias[r])
            att, lse = attend(scores, kept_v[r, :, head_cols(kv)])
            for g in range(GROUP):
                head = kv * GROUP + g
                part = slice(g * MEN, (g + 1) * MEN)
                out_all[r, :, head_cols(head)] = att[part]
                tile = jnp.where(lane == head, lse[part], tile)
        out_all[r, :, COLS:WIDE] = tile
        return carry

    lax.fori_loop(0, NX, step, 0)
    for r, out in enumerate(outs):
        out[...] = out_all[r]
    for r in range(NX):
        for copy in kept_copies(r):
            copy.wait()


def node_backward(q0, q1, q2, q3, g0, g1, g2, g3, bias, keys, values, *refs):
    outs, q_all, g_all, out_all = refs[:NX], *refs[NX:]
    for r, (queries, message) in enumerate(zip((q0, q1, q2, q3), (g0, g1, g2, g3))):
        q_all[r] = queries[...]
        g_all[r] = message[...]

    def step(r, carry):
        lse, center = unpack_numbers(g_all[r, :, COLS:WIDE].astype(F32))
        for kv in range(KV):
            q = stack_heads(q_all.at[r], kv, slice(None))
            grad = stack_heads(g_all.at[r], kv, slice(None))
            key = keys[r, :, head_cols(kv)]
            scores = masked(dot(q, key, NT) * SCALE, bias[r])
            probs = jnp.exp(scores - stack_numbers(lse, kv))
            grad_probs = dot(grad, values[r, :, head_cols(kv)], NT)
            low = (probs * (grad_probs - stack_numbers(center, kv))).astype(BF16)
            grad_q = (dot(low, key) * SCALE).astype(BF16)
            for g in range(GROUP):
                out_all[r, :, head_cols(kv * GROUP + g)] = grad_q[g * MEN : (g + 1) * MEN]
        return carry

    lax.fori_loop(0, NX, step, 0)
    for r, out in enumerate(outs):
        out[...] = out_all[r]


def entity_forward(own, y1, y2, y3, local, table, ids, out_att, out_lse, out_logits):
    parts = (own, y1, y2, y3, local)
    lses = [part[:, COLS:WIDE] for part in parts]
    top = functools.reduce(jnp.maximum, lses)
    weights = [jnp.exp(lse - top) for lse in lses]
    total = functools.reduce(jnp.add, weights)
    out_lse[...] = top + jnp.log(total)
    weights = [weight / total for weight in weights]
    lows = []
    for head in range(HEADS):
        att = functools.reduce(
            jnp.add, [part[:, head_cols(head)] * w[:, head : head + 1] for part, w in zip(parts, weights)]
        )
        out_att[:, head_cols(head)] = att
        lows.append(att.astype(BF16))
    every = dot(jnp.concatenate(lows, 1), table[...], NT)
    entity = lax.broadcasted_iota(jnp.int32, every.shape, 1)
    lane = lax.broadcasted_iota(jnp.int32, (MEN, 128), 1)
    logits = jnp.zeros((MEN, 128), F32)
    for k in range(ids.shape[1]):
        picked = jnp.sum(jnp.where(entity == ids[:, k : k + 1], every, 0.0), axis=1, keepdims=True)
        logits = jnp.where(lane == k, picked, logits)
    out_logits[...] = logits


def log_softmax(values, live):
    values = jnp.where(live, values, LOW)
    values = values - jnp.max(values, axis=1, keepdims=True)
    return values - jnp.log(jnp.sum(jnp.exp(values), axis=1, keepdims=True))


def teacher_kernel(teacher, out_log, out):
    live = lax.broadcasted_iota(jnp.int32, (MEN, 128), 1) < TOPK
    log_target = log_softmax(teacher[...], live)
    out_log[...] = log_target
    out[...] = jnp.where(live, jnp.exp(log_target), 0.0)


def entity_backward(l0, l1, l2, l3, log_target_ref, target_ref, ids, table, att, lse, out, out_div):
    count = ids.shape[1]
    lane = lax.broadcasted_iota(jnp.int32, (MEN, 128), 1)
    live = lane < count
    log_model = log_softmax((l0[...] + l2[...]) + (l1[...] + l3[...]), live)
    log_target = log_target_ref[...]
    target = target_ref[...]
    terms = jnp.where(live, target * (log_target - log_model), 0.0)
    out_div[...] = jnp.broadcast_to(jnp.sum(terms, axis=1, keepdims=True), (MEN, 128))
    grad_logits = jnp.where(live, jnp.exp(log_model), 0.0) - target
    entity = lax.broadcasted_iota(jnp.int32, (MEN, table.shape[0]), 1)
    spread = jnp.zeros((MEN, table.shape[0]), F32)
    for k in range(count):
        spread = jnp.where(entity == ids[:, k : k + 1], grad_logits[:, k : k + 1], spread)
    high, middle, low = three_parts(spread)
    three = dot(jnp.concatenate([high, middle, low], 0).astype(BF16), table[...])
    grad = (three[:MEN] + three[MEN : 2 * MEN] + three[2 * MEN :]).astype(BF16)
    out[:, :COLS] = grad
    center = jnp.zeros((MEN, 128), F32)
    for head in range(HEADS):
        product = grad[:, head_cols(head)].astype(F32) * att[:, head_cols(head)]
        center = jnp.where(lane == head, jnp.sum(product, axis=1, keepdims=True), center)
    numbers = jnp.zeros((MEN, 128), F32)
    for i, part in enumerate(three_parts(jnp.where(lane < HEADS, lse[...], 0.0)) + three_parts(center)):
        numbers = numbers + (pltpu.roll(part, i * HEADS, 1) if i else part)
    out[:, COLS:WIDE] = numbers.astype(BF16)


def owner_kernel(counts, has_start, place, mine, theirs, *refs):
    refs = list(refs)
    start = (refs.pop(0), refs.pop(0)) if has_start else None
    qs = [refs.pop(0) for _ in range(counts[0])]
    gs = [refs.pop(0) for _ in range(counts[1])]
    out_k, out_v, q_all, g_all, keys, values = refs
    for side, rows in ((mine, slice(0, OWN)), (theirs, slice(OWN, CHIP))):
        keys[rows, :] = side[0]
        values[rows, :] = side[1]
    for parts, every in ((qs, q_all), (gs, g_all)):
        at = 0
        for part in parts:
            every[at : at + part.shape[0], :] = part[...]
            at += part.shape[0]
    total = g_all.shape[0] // 128
    if start is None:
        out_k[...] = jnp.zeros_like(out_k)
        out_v[...] = jnp.zeros_like(out_v)
    else:
        out_k[...] = start[0][...]
        out_v[...] = start[1][...]
    blocks = CHIP // DBLK
    block = lax.broadcasted_iota(jnp.int32, (blocks, 128), 0)
    block = block + jnp.where(block < BLK, place[0], place[1] - BLK)
    group = lax.broadcasted_iota(jnp.int32, (blocks, 128), 1) // MEN_CH

    def step(i, carry):
        rows = pl.ds(pl.multiple_of(i * 128, 128), 128)
        listed = jnp.zeros((blocks, 128), F32)
        for r in range(NX):
            tile = q_all[pl.ds(pl.multiple_of(i * 128 + r * MEN, MEN), 16), COLS:WIDE].astype(F32)
            asked = (tile[0:2] * BLK + tile[2:4]).astype(jnp.int32)
            for t in range(2):
                hit = jnp.where(asked[t : t + 1] == block, 1.0, 0.0)
                hit = jnp.max(hit, axis=1, keepdims=True)
                listed = jnp.where(group == 2 * r + t, hit, listed)
        numbers = jnp.transpose(g_all[rows, COLS:WIDE].astype(F32))
        lse = numbers[0:8] + numbers[8:16] + numbers[16:24]
        center = numbers[24:32] + numbers[32:40] + numbers[40:48]
        for kv in range(KV):
            heads = range(kv * GROUP, (kv + 1) * GROUP)
            q = jnp.concatenate([q_all[rows, head_cols(h)] for h in heads], 0)
            g = jnp.concatenate([g_all[rows, head_cols(h)] for h in heads], 0)
            offset = jnp.concatenate([jnp.where(listed > 0.5, -lse[h : h + 1], LOW) for h in heads], 1)
            middle = jnp.concatenate([center[h : h + 1] for h in heads], 1)
            scores = dot(keys[:, head_cols(kv)], q, NT) * SCALE
            scores = scores.reshape(blocks, DBLK, scores.shape[1]) + offset[:, None, :]
            probs = jnp.exp(scores.reshape(CHIP, scores.shape[2]))
            grad_probs = dot(values[:, head_cols(kv)], g, NT)
            low = (probs * (grad_probs - middle)).astype(BF16)
            out_v[:, head_cols(kv)] += dot(probs.astype(BF16), g)
            out_k[:, head_cols(kv)] += dot(low, q)
        return carry

    lax.fori_loop(0, total, step, 0)


def owner_part(place, mine, theirs, start, qs, gs):
    shape = jax.ShapeDtypeStruct((CHIP, KV * HEAD_DIM), F32)
    rows = sum(g.shape[0] for g in gs)
    operands = [place, mine, theirs] + list(start or ()) + list(qs) + list(gs)
    message = pltpu.VMEM((rows, WIDE), BF16)
    stored = pltpu.VMEM((CHIP, KV * HEAD_DIM), BF16)
    return call(
        functools.partial(owner_kernel, (len(qs), len(gs)), start is not None),
        (shape, shape),
        operands,
        smem=(0,),
        scratch=[message, message, stored, stored],
        flops=8 * rows * HEADS * CHIP * HEAD_DIM,
        moved=4 * rows * WIDE + 12 * CHIP * KV * HEAD_DIM,
    )


def join_kernel(m0, m1, m2, m3, out):
    for r, part in enumerate((m0, m1, m2, m3)):
        out[r * MEN : (r + 1) * MEN, :] = part[...]


def join(parts):
    (out,) = call(join_kernel, [jax.ShapeDtypeStruct((NX * MEN, WIDE), BF16)], parts, moved=6 * 10**5)
    return out


def both_ways(up, down):
    return shift_z(up, 1), shift_z(down, -1)


def last_way(up, down):
    half = up.shape[0] // 2
    return shift_z(up[:half], 1), shift_z(down[half:], -1)


def per_device(
    mention_queries,
    pack_keys,
    pack_values,
    desc_keys,
    desc_values,
    desc_lengths,
    block_lists,
    block_home,
    mention_positions,
    entity_table,
    teacher_ids,
    teacher_logits,
):
    my_x, my_z, my_c = (lax.axis_index(name) for name in SEQ)
    me = (my_x * NZ + my_z) * NC + my_c
    shape = jax.ShapeDtypeStruct
    hold = lax.optimization_barrier

    own = jnp.stack([desc_keys.reshape(OWN, -1), desc_values.reshape(OWN, -1)])
    ring = [both_ways(own, own)]

    number = jnp.arange(block_home.shape[0])
    home = jnp.sum(jnp.where(block_lists[:, :, None] == number, block_home, 0), 2)
    lengths = jnp.sum(jnp.where(home[:, :, None] == number, desc_lengths, 0), 2)
    extra = jnp.pad(jnp.concatenate([home // BLK, home % BLK, lengths], 0), ((0, 0), (0, 128 - LISTED // 2)), constant_values=255)
    extra = jnp.pad(extra, ((0, MEN - extra.shape[0]), (0, 0))).astype(BF16)
    positions = mention_positions.reshape(MEN, 1)
    teacher = jnp.pad(teacher_logits, ((0, 0), (0, 128 - teacher_logits.shape[1])))
    my_lengths = lax.dynamic_slice_in_dim(desc_lengths, me * BLK, BLK)
    ring[0], mention_queries, extra, my_lengths = hold((ring[0], mention_queries, extra, my_lengths))
    ring.append(both_ways(*ring[0]))
    queries = lax.all_to_all(mention_queries, "head", split_axis=1, concat_axis=0, tiled=True)
    query_row = jnp.concatenate([queries, extra], 1)
    q = [query_row] + [shift_x(query_row, d) for d in (1, 2, 3)]

    ring[1], pack_keys, q, own, positions, teacher, teacher_ids = hold(
        (ring[1], pack_keys, q, own, positions, teacher, teacher_ids)
    )
    ring.append(both_ways(*ring[1]))
    other = swap(own)
    across = [(swap(ring[0][0]), swap(ring[0][1]))]
    (pack,) = call(
        pack_kernel, [shape((NH, 2 * PART, KV * HEAD_DIM), BF16)], [pack_keys, pack_values], moved=2 * 10**6
    )
    pack = lax.all_to_all(pack, "head", split_axis=0, concat_axis=0, tiled=True)
    row, bias = call(
        slot_kernel,
        [shape((SLOTS, 128), jnp.int32), shape((NX, 2, SPAN), F32)],
        [jnp.stack([my_x, my_z, my_c])] + q,
        smem=(0,),
        flops=10**9,
        moved=10**5,
    )
    ring[2], row, bias, other, across[0] = hold((ring[2], row, bias, other, across[0]))
    far = [shift_z(ring[2][0][0], 1), shift_z(ring[2][1][1], -1)]
    across.append((swap(ring[1][0]), swap(ring[1][1])))
    q_mine = join(q)
    far, q_mine, across[1] = hold((far, q_mine, across[1]))
    q_ring = [both_ways(q_mine, q_mine)]
    across.append((swap(ring[2][0]), swap(ring[2][1])))
    far_across = [swap(piece) for piece in far]

    gathered = shape((NX, SPAN, KV * HEAD_DIM), BF16)
    kept = pltpu.VMEM(gathered.shape, BF16)
    pieces = [own, other]
    for side in (0, 1):
        for step in range(3):
            pieces += [ring[step][side], across[step][side]]
    pieces += [far[0], far_across[0], far[1], far_across[1]]
    *parts, got_k, got_v = call(
        node_forward,
        [shape((MEN, WIDE), F32)] * NX + [gathered, gathered],
        [row] + q + [bias] + pieces,
        smem=(0,),
        anywhere=range(6, 24),
        far_outs=(4, 5),
        scratch=[
            pltpu.VMEM((2 * NZ * CHIP, KV * HEAD_DIM), BF16),
            kept,
            kept,
            pltpu.VMEM((NX, MEN, WIDE), BF16),
            pltpu.VMEM((NX, MEN, WIDE), F32),
            pltpu.SemaphoreType.DMA((4 * NZ,)),
            pltpu.SemaphoreType.DMA((2 * NX,)),
        ],
        flops=10**9,
        moved=10**7,
        vmem=60 * 1024 * 1024,
    )
    parts, pack, q_ring[0] = hold((parts, pack, q_ring[0]))
    returned = [shift_x(parts[d], -d) for d in (1, 2, 3)]
    (local_part,) = call(
        self_forward, [shape((MEN, WIDE), F32)], [queries, pack, positions], flops=10**9, moved=2 * 10**6
    )
    q_ring.append(both_ways(*q_ring[0]))
    att, lse, logits = call(
        entity_forward,
        [shape((MEN, COLS), F32), shape((MEN, 128), F32), shape((MEN, 128), F32)],
        [parts[0]] + returned + [local_part, entity_table, teacher_ids],
        flops=10**8,
        moved=3 * 10**6,
    )
    everyone = [logits] + [shift_head(logits, d) for d in (1, 2, 3)]
    log_target, target = call(teacher_kernel, [shape((MEN, 128), F32)] * 2, [teacher])
    q_ring.append(both_ways(*q_ring[1]))
    message, divergence_wide = call(
        entity_backward,
        [shape((MEN, WIDE), BF16), shape((MEN, 128), F32)],
        everyone + [log_target, target, teacher_ids, entity_table, att, lse],
        flops=3 * 10**8,
        moved=3 * 10**6,
    )
    g = [message] + [shift_x(message, d) for d in (1, 2, 3)]

    pack_shape = shape((2 * STRETCH, KV * HEAD_DIM), BF16)
    local_q, grad_pack_keys, grad_pack_values = call(
        self_backward,
        [shape((MEN, COLS), F32), pack_shape, pack_shape],
        [queries, pack, positions, message],
        flops=10**9,
        moved=4 * 10**6,
    )
    g, local_q = hold((g, local_q))

    place = jnp.stack([me * BLK, (me + 1 - 2 * my_c) * BLK])

    def owner(start, qs, gs):
        return owner_part(place, own, other, start, qs, gs)

    g_mine = join(g)
    g_ring = [both_ways(g_mine, g_mine)]
    node_q = call(
        node_backward,
        [shape((MEN, COLS), BF16)] * NX,
        q + g + [bias, got_k, got_v],
        scratch=[pltpu.VMEM((NX, MEN, WIDE), BF16)] * 2 + [pltpu.VMEM((NX, MEN, COLS), BF16)],
        flops=10**9,
        moved=6 * 10**6,
        vmem=60 * 1024 * 1024,
    )
    g_ring[0], node_q, q_ring[2] = hold((g_ring[0], node_q, q_ring[2]))
    g_ring.append(both_ways(*g_ring[0]))
    back_q = [shift_x(node_q[d], -d) for d in (1, 2, 3)]
    g_ring[1], back_q, g_ring[0] = hold((g_ring[1], back_q, g_ring[0]))
    g_ring.append(both_ways(*g_ring[1]))
    q_far = shift_z(q_ring[2][0], 1)
    sums = owner(None, [q_mine, *q_ring[0]], [g_mine, *g_ring[0]])
    sums = owner(sums, q_ring[1], g_ring[1])
    g_ring[2], sums, divergence = hold((g_ring[2], sums, divergence_wide[:, 0]))
    g_ring.append(last_way(*g_ring[2]))
    sums = owner(sums, q_ring[2], g_ring[2])
    grad_queries = functools.reduce(
        jnp.add, [part.astype(F32) for part in [node_q[0]] + back_q], local_q
    ).astype(BF16)
    g_ring[3], sums = hold((g_ring[3], sums))
    sums = owner(sums, [q_far], g_ring[3])
    both = jnp.stack(sums)
    total = both[:, :OWN] + swap(both[:, OWN:].astype(BF16)).astype(F32)
    visible = (jnp.arange(DBLK)[None, :] < my_lengths[:, None])[:, :, None]
    total = total.reshape(2, BLK, DBLK, KV * HEAD_DIM)
    grad_desc_keys = jnp.where(visible, total[0] * SCALE, 0.0)
    grad_desc_values = jnp.where(visible, total[1], 0.0)
    return (
        grad_queries,
        grad_pack_keys,
        grad_pack_values,
        grad_desc_keys,
        grad_desc_values,
        divergence,
    )


def solution(mesh):
    axes = Mesh(mesh.devices.reshape(NX, NZ, NC, NH), SEQ + ("head",))
    placed = (
        P(SEQ + ("head",), None),
        P(SEQ + ("head",), None),
        P(SEQ + ("head",), None),
        P(SEQ, None, "head"),
        P(SEQ, None, "head"),
        P(),
        P(SEQ, None),
        P(),
        P(SEQ),
        P(None, "head"),
        P(SEQ, None),
        P(SEQ, None),
    )
    return jax.shard_map(
        per_device,
        mesh=axes,
        in_specs=placed,
        out_specs=(
            P(SEQ, "head"),
            P(SEQ, "head"),
            P(SEQ, "head"),
            P(SEQ, None, "head"),
            P(SEQ, None, "head"),
            P(SEQ),
        ),
        check_vma=False,
    )
```

```python
import functools

import jax
import jax.numpy as jnp
from jax import lax
from jax.experimental import pallas as pl
from jax.experimental.pallas import tpu as pltpu
from jax.sharding import Mesh
from jax.sharding import PartitionSpec as P

HEAD_DIM = 128
SCALE = HEAD_DIM ** (-0.5)
NX, NZ, NC, NH = 4, 8, 2, 4
GROUP = 4
KV = 2
HEADS = GROUP * KV
COLS = HEADS * HEAD_DIM
WIDE = COLS + 128
DBLK = 32
BLK = 8
OWN = BLK * DBLK
CHIP = NC * OWN
MEN = 32
MEN_CH = 16
STRETCH = 512
PART = 256
LISTED = 64
TOPK = 16
SLOTS = 2 * NZ * NC
SPAN = SLOTS * DBLK
LOW = -1e30
LOG2E = 1.4426950408889634
F32 = jnp.float32
BF16 = jnp.bfloat16
NT = (((1,), (1,)), ((), ()))
TN = (((0,), (0,)), ((), ()))
VMEM_BYTES = 40 * 1024 * 1024
SEQ = ("x", "z", "core")


def pairs(move):
    out = []
    for x in range(NX):
        for z in range(NZ):
            for c in range(NC):
                tx, tz, tc = move(x, z, c)
                out.append(((x * NZ + z) * NC + c, ((tx % NX) * NZ + tz % NZ) * NC + tc))
    return out


def shift_x(value, step):
    return lax.ppermute(value, SEQ, pairs(lambda x, z, c: (x + step, z, c)))


def shift_z(value, step):
    return lax.ppermute(value, SEQ, pairs(lambda x, z, c: (x, z + step, c)))


def swap(value):
    return lax.ppermute(value, SEQ, pairs(lambda x, z, c: (x, z, 1 - c)))


def shift_head(value, step):
    return lax.ppermute(value, "head", [(i, (i + step) % NH) for i in range(NH)])


def dot(left, right, dims=(((1,), (0,)), ((), ()))):
    return lax.dot_general(left, right, dims, preferred_element_type=F32)


def head_cols(head):
    return slice(head * HEAD_DIM, (head + 1) * HEAD_DIM)


def call(kernel, out_shape, operands, smem=(), anywhere=(), far_outs=(), scratch=(), flops=0, moved=0, vmem=VMEM_BYTES):
    space = lambda i: pltpu.SMEM if i in smem else pl.ANY if i in anywhere else pltpu.VMEM
    specs = [pl.BlockSpec(memory_space=space(i)) for i in range(len(operands))]
    outs = [pl.BlockSpec(memory_space=pltpu.HBM if i in far_outs else pltpu.VMEM) for i in range(len(out_shape))]
    return pl.pallas_call(
        kernel,
        out_shape=tuple(out_shape),
        in_specs=specs,
        out_specs=tuple(outs),
        scratch_shapes=list(scratch),
        compiler_params=pltpu.CompilerParams(vmem_limit_bytes=vmem),
        cost_estimate=pl.CostEstimate(flops=flops, bytes_accessed=moved, transcendentals=0),
    )(*operands)


def stack_heads(ref, kv, rows):
    return jnp.concatenate([ref[rows, head_cols(kv * GROUP + g)] for g in range(GROUP)], 0)


def stack_numbers(tile, kv):
    return jnp.concatenate([tile[:, kv * GROUP + g : kv * GROUP + g + 1] for g in range(GROUP)], 0)


def unpack_numbers(tile):
    first = tile + pltpu.roll(tile, 120, 1) + pltpu.roll(tile, 112, 1)
    second = pltpu.roll(tile, 104, 1) + pltpu.roll(tile, 96, 1) + pltpu.roll(tile, 88, 1)
    return first, second


def three_parts(value):
    high = value.astype(BF16).astype(F32)
    rest = value - high
    middle = rest.astype(BF16).astype(F32)
    return high, middle, (rest - middle).astype(BF16).astype(F32)


def attend(scores, values):
    top = jnp.max(scores, axis=1, keepdims=True)
    weights = jnp.exp(scores - top)
    total = jnp.sum(weights, axis=1, keepdims=True)
    return dot(weights.astype(BF16), values) / total, top + jnp.log(total)


def pack_kernel(keys, values, out):
    for h in range(NH):
        cols = slice(h * KV * HEAD_DIM, (h + 1) * KV * HEAD_DIM)
        out[h, :PART, :] = keys[:, cols]
        out[h, PART:, :] = values[:, cols]


def own_rows(ref, t, which, kv):
    span = slice(which * PART, (which + 1) * PART)
    return jnp.concatenate([ref[2 * t, span, head_cols(kv)], ref[2 * t + 1, span, head_cols(kv)]], 0)


def self_forward(queries, pack, positions, out):
    lane = lax.broadcasted_iota(jnp.int32, (MEN_CH, 128), 1)
    token = lax.broadcasted_iota(jnp.int32, (GROUP * MEN_CH, STRETCH), 1)
    for t in range(2):
        rows = slice(t * MEN_CH, (t + 1) * MEN_CH)
        place = jnp.concatenate([positions[rows, :]] * GROUP, 0)
        tile = jnp.zeros((MEN_CH, 128), F32)
        for kv in range(KV):
            q = stack_heads(queries, kv, rows)
            scores = dot(q, own_rows(pack, t, 0, kv), NT) * SCALE
            scores = jnp.where(token <= place, scores, LOW)
            att, lse = attend(scores, own_rows(pack, t, 1, kv))
            for g in range(GROUP):
                head = kv * GROUP + g
                part = slice(g * MEN_CH, (g + 1) * MEN_CH)
                out[rows, head_cols(head)] = att[part]
                tile = jnp.where(lane == head, lse[part], tile)
        out[rows, COLS:WIDE] = tile


def self_backward(queries, pack, positions, message, out_q, out_k, out_v):
    token = lax.broadcasted_iota(jnp.int32, (GROUP * MEN_CH, STRETCH), 1)
    for t in range(2):
        rows = slice(t * MEN_CH, (t + 1) * MEN_CH)
        span = slice(t * STRETCH, (t + 1) * STRETCH)
        place = jnp.concatenate([positions[rows, :]] * GROUP, 0)
        lse, center = unpack_numbers(message[rows, COLS:WIDE].astype(F32))
        for kv in range(KV):
            q = stack_heads(queries, kv, rows)
            grad = stack_heads(message, kv, rows)
            key = own_rows(pack, t, 0, kv)
            value = own_rows(pack, t, 1, kv)
            scores = dot(q, key, NT) * SCALE
            scores = jnp.where(token <= place, scores, LOW)
            probs = jnp.exp(scores - stack_numbers(lse, kv))
            grad_scores = probs * (dot(grad, value, NT) - stack_numbers(center, kv))
            low = grad_scores.astype(BF16)
            grad_q = dot(low, key) * SCALE
            for g in range(GROUP):
                out_q[rows, head_cols(kv * GROUP + g)] = grad_q[g * MEN_CH : (g + 1) * MEN_CH]
            out_k[span, head_cols(kv)] = (dot(low, q, TN) * SCALE).astype(BF16)
            out_v[span, head_cols(kv)] = dot(probs.astype(BF16), grad, TN).astype(BF16)


def masked(scores, bias):
    four = scores.reshape(GROUP, 2, MEN_CH, SPAN) + bias[None, :, None, :]
    return four.reshape(GROUP * MEN, SPAN)


def slot_kernel(place, q0, q1, q2, q3, out_rows, out_bias):
    lane = lax.broadcasted_iota(jnp.int32, (2, 128), 1)
    before = lax.broadcasted_iota(jnp.int32, (128, 128), 0) < lax.broadcasted_iota(jnp.int32, (128, 128), 1)
    before = jnp.where(before, 1.0, 0.0).astype(BF16)
    slot = lax.broadcasted_iota(jnp.int32, (SLOTS, 128), 0)
    wide = lax.broadcasted_iota(jnp.int32, (SLOTS, 128), 1)
    spread = lax.broadcasted_iota(jnp.int32, (SLOTS, SPAN), 1) // DBLK
    spread = spread == lax.broadcasted_iota(jnp.int32, (SLOTS, SPAN), 0)
    spread = jnp.where(spread, 1.0, 0.0).astype(BF16)
    row_in = (lax.broadcasted_iota(jnp.int32, (1, SPAN), 1) % DBLK).astype(F32)
    rows = jnp.zeros((SLOTS, 128), jnp.int32)
    for r, queries in enumerate((q0, q1, q2, q3)):
        tile = queries[0:16, COLS:WIDE]
        numbers = tile.astype(F32).astype(jnp.int32)
        owner, local = numbers[0:2], numbers[2:4]
        match = (owner // (NZ * NC) == place[0]) & (lane < LISTED // 2)
        ones = jnp.where(match, 1.0, 0.0)
        rank = dot(ones.astype(BF16), before)
        first = jnp.sum(ones[0:1], axis=1, keepdims=True)
        rank = jnp.concatenate([rank[0:1], rank[1:2] + first], 0).astype(jnp.int32)
        away = ((owner // NC) % NZ + (NZ - place[1])) % NZ
        row = away * CHIP + ((owner + place[2]) % NC) * OWN + local * DBLK
        column = jnp.zeros((SLOTS, 1), jnp.int32)
        for t in range(2):
            chosen = (slot == rank[t : t + 1]) & (ones[t : t + 1] > 0.5)
            column = column + jnp.sum(jnp.where(chosen, row[t : t + 1], 0), axis=1, keepdims=True)
            live = dot(tile, jnp.where(chosen, 1.0, 0.0).astype(BF16), NT)
            live = dot(live.astype(BF16), spread)[4 + t : 5 + t]
            out_bias[r, t : t + 1, :] = jnp.where(row_in < live, 0.0, LOW)
        rows = jnp.where(wide == r, column, rows)
    out_rows[...] = rows


def node_forward(row, q0, q1, q2, q3, bias, *refs):
    near, far = refs[:14], refs[14:18]
    outs, out_k, out_v, pool, kept_k, kept_v, q_all, out_all, sems_in, sems_out = refs[18:22], *refs[22:]
    half = NZ * CHIP
    pieces = []
    for i, piece in enumerate(near):
        away, other = ((0, 7, 6, 5, 1, 2, 3)[i // 2], i % 2)
        pieces += [(piece.at[0], 2 * away + other), (piece.at[1], 2 * (NZ + away) + other)]
    pieces += [(far[0], 8), (far[1], 9), (far[2], 2 * NZ + 8), (far[3], 2 * NZ + 9)]
    copies = [
        pltpu.make_async_copy(piece, pool.at[pl.ds(i * OWN, OWN), :], sems_in.at[i]) for piece, i in pieces
    ]
    for copy in copies:
        copy.start()
    for copy in copies:
        copy.wait()
    for r, queries in enumerate((q0, q1, q2, q3)):
        q_all[r] = queries[...]
    lane = lax.broadcasted_iota(jnp.int32, (MEN, 128), 1)

    def kept_copies(r):
        return (
            pltpu.make_async_copy(kept_k.at[r], out_k.at[r], sems_out.at[2 * r]),
            pltpu.make_async_copy(kept_v.at[r], out_v.at[r], sems_out.at[2 * r + 1]),
        )

    def step(r, carry):
        for j in range(SLOTS):
            rows = slice(j * DBLK, (j + 1) * DBLK)
            kept_k[r, rows, :] = pool[pl.ds(pl.multiple_of(row[j, r], DBLK), DBLK), :]
            kept_v[r, rows, :] = pool[pl.ds(pl.multiple_of(half + row[j, r], DBLK), DBLK), :]
        for copy in kept_copies(r):
            copy.start()
        tile = jnp.zeros((MEN, 128), F32)
        for kv in range(KV):
            q = stack_heads(q_all.at[r], kv, slice(None))
            scores = masked(dot(q, kept_k[r, :, head_cols(kv)], NT) * SCALE, bias[r])
            att, lse = attend(scores, kept_v[r, :, head_cols(kv)])
            for g in range(GROUP):
                head = kv * GROUP + g
                part = slice(g * MEN, (g + 1) * MEN)
                out_all[r, :, head_cols(head)] = att[part]
                tile = jnp.where(lane == head, lse[part], tile)
        out_all[r, :, COLS:WIDE] = tile
        return carry

    lax.fori_loop(0, NX, step, 0)
    for r, out in enumerate(outs):
        out[...] = out_all[r]
    for r in range(NX):
        for copy in kept_copies(r):
            copy.wait()


def node_backward(q0, q1, q2, q3, g0, g1, g2, g3, bias, keys_from, values_from, *refs):
    outs, keys, values, sems = refs[:NX], *refs[NX:]

    def copies(r):
        return (
            pltpu.make_async_copy(keys_from.at[r], keys.at[r], sems.at[2 * r]),
            pltpu.make_async_copy(values_from.at[r], values.at[r], sems.at[2 * r + 1]),
        )

    for copy in copies(0):
        copy.start()
    for r, (queries, message, out) in enumerate(zip((q0, q1, q2, q3), (g0, g1, g2, g3), outs)):
        if r + 1 < NX:
            for copy in copies(r + 1):
                copy.start()
        lse, center = unpack_numbers(message[:, COLS:WIDE].astype(F32))
        for copy in copies(r):
            copy.wait()
        for kv in range(KV):
            q = stack_heads(queries, kv, slice(None))
            grad = stack_heads(message, kv, slice(None))
            key = keys[r, :, head_cols(kv)]
            scores = masked(dot(q, key, NT) * SCALE, bias[r])
            probs = jnp.exp(scores - stack_numbers(lse, kv))
            grad_probs = dot(grad, values[r, :, head_cols(kv)], NT)
            low = (probs * (grad_probs - stack_numbers(center, kv))).astype(BF16)
            grad_q = (dot(low, key) * SCALE).astype(BF16)
            for g in range(GROUP):
                out[:, head_cols(kv * GROUP + g)] = grad_q[g * MEN : (g + 1) * MEN]


def entity_forward(own, y1, y2, y3, local, table, ids, out_att, out_lse, out_logits):
    parts = (own, y1, y2, y3, local)
    lses = [part[:, COLS:WIDE] for part in parts]
    top = functools.reduce(jnp.maximum, lses)
    weights = [jnp.exp(lse - top) for lse in lses]
    total = functools.reduce(jnp.add, weights)
    out_lse[...] = top + jnp.log(total)
    weights = [weight / total for weight in weights]
    lows = []
    for head in range(HEADS):
        att = functools.reduce(
            jnp.add, [part[:, head_cols(head)] * w[:, head : head + 1] for part, w in zip(parts, weights)]
        )
        out_att[:, head_cols(head)] = att
        lows.append(att.astype(BF16))
    every = dot(jnp.concatenate(lows, 1), table[...], NT)
    entity = lax.broadcasted_iota(jnp.int32, every.shape, 1)
    lane = lax.broadcasted_iota(jnp.int32, (MEN, 128), 1)
    logits = jnp.zeros((MEN, 128), F32)
    for k in range(ids.shape[1]):
        picked = jnp.sum(jnp.where(entity == ids[:, k : k + 1], every, 0.0), axis=1, keepdims=True)
        logits = jnp.where(lane == k, picked, logits)
    out_logits[...] = logits


def log_softmax(values, live):
    values = jnp.where(live, values, LOW)
    values = values - jnp.max(values, axis=1, keepdims=True)
    return values - jnp.log(jnp.sum(jnp.exp(values), axis=1, keepdims=True))


def teacher_kernel(teacher, out_log, out):
    live = lax.broadcasted_iota(jnp.int32, (MEN, 128), 1) < TOPK
    log_target = log_softmax(teacher[...], live)
    out_log[...] = log_target
    out[...] = jnp.where(live, jnp.exp(log_target), 0.0)


def entity_backward(l0, l1, l2, l3, log_target_ref, target_ref, ids, table, att, lse, out, out_div):
    count = ids.shape[1]
    lane = lax.broadcasted_iota(jnp.int32, (MEN, 128), 1)
    live = lane < count
    log_model = log_softmax((l0[...] + l2[...]) + (l1[...] + l3[...]), live)
    log_target = log_target_ref[...]
    target = target_ref[...]
    terms = jnp.where(live, target * (log_target - log_model), 0.0)
    out_div[...] = jnp.broadcast_to(jnp.sum(terms, axis=1, keepdims=True), (MEN, 128))
    grad_logits = jnp.where(live, jnp.exp(log_model), 0.0) - target
    entity = lax.broadcasted_iota(jnp.int32, (MEN, table.shape[0]), 1)
    spread = jnp.zeros((MEN, table.shape[0]), F32)
    for k in range(count):
        spread = jnp.where(entity == ids[:, k : k + 1], grad_logits[:, k : k + 1], spread)
    high, middle, low = three_parts(spread)
    three = dot(jnp.concatenate([high, middle, low], 0).astype(BF16), table[...])
    grad = (three[:MEN] + three[MEN : 2 * MEN] + three[2 * MEN :]).astype(BF16)
    out[:, :COLS] = grad
    center = jnp.zeros((MEN, 128), F32)
    for head in range(HEADS):
        product = grad[:, head_cols(head)].astype(F32) * att[:, head_cols(head)]
        center = jnp.where(lane == head, jnp.sum(product, axis=1, keepdims=True), center)
    numbers = jnp.zeros((MEN, 128), F32)
    for i, part in enumerate(three_parts(jnp.where(lane < HEADS, lse[...], 0.0)) + three_parts(center)):
        numbers = numbers + (pltpu.roll(part, i * HEADS, 1) if i else part)
    out[:, COLS:WIDE] = numbers.astype(BF16)


def owner_kernel(counts, has_start, place, mine, theirs, *refs):
    refs = list(refs)
    start = (refs.pop(0), refs.pop(0)) if has_start else None
    qs = [refs.pop(0) for _ in range(counts[0])]
    gs = [refs.pop(0) for _ in range(counts[1])]
    out_k, out_v, q_all, g_all, keys, values = refs
    for side, rows in ((mine, slice(0, OWN)), (theirs, slice(OWN, CHIP))):
        keys[rows, :] = side[0]
        values[rows, :] = side[1]
    for parts, every in ((qs, q_all), (gs, g_all)):
        at = 0
        for part in parts:
            every[at : at + part.shape[0], :] = part[...]
            at += part.shape[0]
    total = g_all.shape[0] // 128
    if start is None:
        out_k[...] = jnp.zeros_like(out_k)
        out_v[...] = jnp.zeros_like(out_v)
    else:
        out_k[...] = start[0][...]
        out_v[...] = start[1][...]
    blocks = CHIP // DBLK
    block = lax.broadcasted_iota(jnp.int32, (blocks, 128), 0)
    block = block + jnp.where(block < BLK, place[0], place[1] - BLK)
    group = lax.broadcasted_iota(jnp.int32, (blocks, 128), 1) // MEN_CH

    def step(i, carry):
        rows = pl.ds(pl.multiple_of(i * 128, 128), 128)
        listed = jnp.zeros((blocks, 128), F32)
        for r in range(NX):
            tile = q_all[pl.ds(pl.multiple_of(i * 128 + r * MEN, MEN), 16), COLS:WIDE].astype(F32)
            asked = (tile[0:2] * BLK + tile[2:4]).astype(jnp.int32)
            for t in range(2):
                hit = jnp.where(asked[t : t + 1] == block, 1.0, 0.0)
                hit = jnp.max(hit, axis=1, keepdims=True)
                listed = jnp.where(group == 2 * r + t, hit, listed)
        numbers = jnp.transpose(g_all[rows, COLS:WIDE].astype(F32))
        lse = (numbers[0:8] + numbers[8:16] + numbers[16:24]) * LOG2E
        center = numbers[24:32] + numbers[32:40] + numbers[40:48]
        for kv in range(KV):
            heads = range(kv * GROUP, (kv + 1) * GROUP)
            q = jnp.concatenate([q_all[rows, head_cols(h)] for h in heads], 0)
            g = jnp.concatenate([g_all[rows, head_cols(h)] for h in heads], 0)
            offset = jnp.concatenate([jnp.where(listed > 0.5, -lse[h : h + 1], LOW) for h in heads], 1)
            middle = jnp.concatenate([center[h : h + 1] for h in heads], 1)
            scores = dot(keys[:, head_cols(kv)], q, NT) * (SCALE * LOG2E)
            scores = scores.reshape(blocks, DBLK, scores.shape[1]) + offset[:, None, :]
            probs = jnp.exp2(scores.reshape(CHIP, scores.shape[2]))
            grad_probs = dot(values[:, head_cols(kv)], g, NT)
            low = (probs * (grad_probs - middle)).astype(BF16)
            out_v[:, head_cols(kv)] += dot(probs.astype(BF16), g)
            out_k[:, head_cols(kv)] += dot(low, q)
        return carry

    lax.fori_loop(0, total, step, 0)


def owner_part(place, mine, theirs, start, qs, gs):
    shape = jax.ShapeDtypeStruct((CHIP, KV * HEAD_DIM), F32)
    rows = sum(g.shape[0] for g in gs)
    operands = [place, mine, theirs] + list(start or ()) + list(qs) + list(gs)
    message = pltpu.VMEM((rows, WIDE), BF16)
    stored = pltpu.VMEM((CHIP, KV * HEAD_DIM), BF16)
    return call(
        functools.partial(owner_kernel, (len(qs), len(gs)), start is not None),
        (shape, shape),
        operands,
        smem=(0,),
        scratch=[message, message, stored, stored],
        flops=8 * rows * HEADS * CHIP * HEAD_DIM,
        moved=4 * rows * WIDE + 12 * CHIP * KV * HEAD_DIM,
    )


def join_kernel(m0, m1, m2, m3, out):
    for r, part in enumerate((m0, m1, m2, m3)):
        out[r * MEN : (r + 1) * MEN, :] = part[...]


def join(parts):
    (out,) = call(join_kernel, [jax.ShapeDtypeStruct((NX * MEN, WIDE), BF16)], parts, moved=6 * 10**5)
    return out


def both_ways(up, down):
    return shift_z(up, 1), shift_z(down, -1)


def last_way(up, down):
    half = up.shape[0] // 2
    return shift_z(up[:half], 1), shift_z(down[half:], -1)


def per_device(
    mention_queries,
    pack_keys,
    pack_values,
    desc_keys,
    desc_values,
    desc_lengths,
    block_lists,
    block_home,
    mention_positions,
    entity_table,
    teacher_ids,
    teacher_logits,
):
    my_x, my_z, my_c = (lax.axis_index(name) for name in SEQ)
    me = (my_x * NZ + my_z) * NC + my_c
    shape = jax.ShapeDtypeStruct
    hold = lax.optimization_barrier

    own = jnp.stack([desc_keys.reshape(OWN, -1), desc_values.reshape(OWN, -1)])
    ring = [both_ways(own, own)]

    number = jnp.arange(block_home.shape[0])
    home = jnp.sum(jnp.where(block_lists[:, :, None] == number, block_home, 0), 2)
    lengths = jnp.sum(jnp.where(home[:, :, None] == number, desc_lengths, 0), 2)
    extra = jnp.pad(jnp.concatenate([home // BLK, home % BLK, lengths], 0), ((0, 0), (0, 128 - LISTED // 2)), constant_values=255)
    extra = jnp.pad(extra, ((0, MEN - extra.shape[0]), (0, 0))).astype(BF16)
    positions = mention_positions.reshape(MEN, 1)
    teacher = jnp.pad(teacher_logits, ((0, 0), (0, 128 - teacher_logits.shape[1])))
    my_lengths = lax.dynamic_slice_in_dim(desc_lengths, me * BLK, BLK)
    ring[0], extra, my_lengths = hold((ring[0], extra, my_lengths))
    ring.append(both_ways(*ring[0]))
    queries = lax.all_to_all(mention_queries, "head", split_axis=1, concat_axis=0, tiled=True)
    queries, _ = hold((queries, ring[0]))
    query_row = jnp.concatenate([queries, extra], 1)
    q = [query_row] + [shift_x(query_row, d) for d in (1, 2, 3)]

    queries, pack_keys = hold((queries, pack_keys))
    (pack,) = call(
        pack_kernel,
        [shape((NH, 2 * PART, KV * HEAD_DIM), BF16)],
        [pack_keys, pack_values],
        moved=2 * 10**6,
    )
    ring[1], pack, q, own, positions, teacher, teacher_ids = hold(
        (ring[1], pack, q, own, positions, teacher, teacher_ids)
    )
    ring.append(both_ways(*ring[1]))
    other = swap(own)
    across = [(swap(ring[0][0]), swap(ring[0][1]))]
    pack = lax.all_to_all(pack, "head", split_axis=0, concat_axis=0, tiled=True)
    row, bias = call(
        slot_kernel,
        [shape((SLOTS, 128), jnp.int32), shape((NX, 2, SPAN), F32)],
        [jnp.stack([my_x, my_z, my_c])] + q,
        smem=(0,),
        flops=10**9,
        moved=10**5,
    )
    ring[2], row, bias, other, across[0] = hold((ring[2], row, bias, other, across[0]))
    far = [shift_z(ring[2][0][0], 1), shift_z(ring[2][1][1], -1)]
    across.append((swap(ring[1][0]), swap(ring[1][1])))
    q_mine = join(q)
    far, q_mine, across[1] = hold((far, q_mine, across[1]))
    q_ring = [both_ways(q_mine, q_mine)]
    across.append((swap(ring[2][0]), swap(ring[2][1])))
    far_across = [swap(piece) for piece in far]

    gathered = shape((NX, SPAN, KV * HEAD_DIM), BF16)
    kept = pltpu.VMEM(gathered.shape, BF16)
    pieces = [own, other]
    for side in (0, 1):
        for step in range(3):
            pieces += [ring[step][side], across[step][side]]
    pieces += [far[0], far_across[0], far[1], far_across[1]]
    *parts, got_k, got_v = call(
        node_forward,
        [shape((MEN, WIDE), F32)] * NX + [gathered, gathered],
        [row] + q + [bias] + pieces,
        smem=(0,),
        anywhere=range(6, 24),
        far_outs=(4, 5),
        scratch=[
            pltpu.VMEM((2 * NZ * CHIP, KV * HEAD_DIM), BF16),
            kept,
            kept,
            pltpu.VMEM((NX, MEN, WIDE), BF16),
            pltpu.VMEM((NX, MEN, WIDE), F32),
            pltpu.SemaphoreType.DMA((4 * NZ,)),
            pltpu.SemaphoreType.DMA((2 * NX,)),
        ],
        flops=10**9,
        moved=10**7,
        vmem=60 * 1024 * 1024,
    )
    parts, pack = hold((parts, pack))
    returned = [shift_x(parts[d], -d) for d in (1, 2, 3)]
    (local_part,) = call(
        self_forward, [shape((MEN, WIDE), F32)], [queries, pack, positions], flops=10**9, moved=2 * 10**6
    )
    q_ring.append(both_ways(*q_ring[0]))
    att, lse, logits = call(
        entity_forward,
        [shape((MEN, COLS), F32), shape((MEN, 128), F32), shape((MEN, 128), F32)],
        [parts[0]] + returned + [local_part, entity_table, teacher_ids],
        flops=2 * 10**10,
        moved=3 * 10**6,
    )
    everyone = [logits] + [shift_head(logits, d) for d in (1, 2, 3)]
    log_target, target = call(teacher_kernel, [shape((MEN, 128), F32)] * 2, [teacher])
    q_ring.append(both_ways(*q_ring[1]))
    message, divergence_wide = call(
        entity_backward,
        [shape((MEN, WIDE), BF16), shape((MEN, 128), F32)],
        everyone + [log_target, target, teacher_ids, entity_table, att, lse],
        flops=2 * 10**10,
        moved=3 * 10**6,
    )
    g = [message] + [shift_x(message, d) for d in (1, 2, 3)]

    pack_shape = shape((2 * STRETCH, KV * HEAD_DIM), BF16)
    local_q, grad_pack_keys, grad_pack_values = call(
        self_backward,
        [shape((MEN, COLS), F32), pack_shape, pack_shape],
        [queries, pack, positions, message],
        flops=2 * 10**10,
        moved=4 * 10**6,
    )
    g, local_q, q_ring[2] = hold((g, local_q, q_ring[2]))

    place = jnp.stack([me * BLK, (me + 1 - 2 * my_c) * BLK])

    def owner(start, qs, gs):
        return owner_part(place, own, other, start, qs, gs)

    g_mine = join(g)
    g_ring = [both_ways(g_mine, g_mine)]
    node_q = call(
        node_backward,
        [shape((MEN, COLS), BF16)] * NX,
        q + g + [bias, got_k, got_v],
        anywhere=(9, 10),
        scratch=[kept, kept, pltpu.SemaphoreType.DMA((2 * NX,))],
        flops=10**9,
        moved=6 * 10**6,
    )
    g_ring[0], node_q = hold((g_ring[0], node_q))
    g_ring.append(both_ways(*g_ring[0]))
    back_q = [shift_x(node_q[d], -d) for d in (1, 2, 3)]
    g_ring[1], back_q, g_ring[0] = hold((g_ring[1], back_q, g_ring[0]))
    g_ring.append(both_ways(*g_ring[1]))
    q_far = shift_z(q_ring[2][0], 1)
    sums = owner(None, [q_mine, *q_ring[0]], [g_mine, *g_ring[0]])
    sums = owner(sums, q_ring[1], g_ring[1])
    g_ring[2], sums, divergence = hold((g_ring[2], sums, divergence_wide[:, 0]))
    g_ring.append(last_way(*g_ring[2]))
    sums = owner(sums, q_ring[2], g_ring[2])
    grad_queries = functools.reduce(
        jnp.add, [part.astype(F32) for part in [node_q[0]] + back_q], local_q
    ).astype(BF16)
    g_ring[3], sums = hold((g_ring[3], sums))
    sums = owner(sums, [q_far], g_ring[3])
    both = jnp.stack(sums)
    total = both[:, :OWN] + swap(both[:, OWN:].astype(BF16)).astype(F32)
    visible = (jnp.arange(DBLK)[None, :] < my_lengths[:, None])[:, :, None]
    total = total.reshape(2, BLK, DBLK, KV * HEAD_DIM)
    grad_desc_keys = jnp.where(visible, total[0] * SCALE, 0.0)
    grad_desc_values = jnp.where(visible, total[1], 0.0)
    return (
        grad_queries,
        grad_pack_keys,
        grad_pack_values,
        grad_desc_keys,
        grad_desc_values,
        divergence,
    )


def solution(mesh):
    axes = Mesh(mesh.devices.reshape(NX, NZ, NC, NH), SEQ + ("head",))
    placed = (
        P(SEQ + ("head",), None),
        P(SEQ + ("head",), None),
        P(SEQ + ("head",), None),
        P(SEQ, None, "head"),
        P(SEQ, None, "head"),
        P(),
        P(SEQ, None),
        P(),
        P(SEQ),
        P(None, "head"),
        P(SEQ, None),
        P(SEQ, None),
    )
    return jax.shard_map(
        per_device,
        mesh=axes,
        in_specs=placed,
        out_specs=(
            P(SEQ, "head"),
            P(SEQ, "head"),
            P(SEQ, "head"),
            P(SEQ, None, "head"),
            P(SEQ, None, "head"),
            P(SEQ),
        ),
        check_vma=False,
    )
```
